256 devices in a mesh: blk: 64 (over y, z, core), rep: 4 (over x).
Axes of the slice: x: 4, y: 4, z: 8, core: 2. Of those that a mesh axis runs over, the one named last changes fastest.
Arguments:
- sim: bfloat16 [131072, 512], P(('blk', 'rep')), may hold values from -48 to 48, as said below
- real: bfloat16 [131072, 512], P('blk', 'rep'), may hold values from -48 to 48, as said below
- pair_real: int32 [512, 16], P(('blk', 'rep')), may hold values from 0 to 511, as said below
- pair_count: int32 [512], P(('blk', 'rep')), may hold values from 2 to 16, as said below
Outputs:
- pull: float32 [131072, 512], P(('blk', 'rep'))
- sim_potential: float32 [131072], P(('blk', 'rep'))
- real_potential: float32 [131072], P('blk')
The draws below stay inside these ranges and needn't reach their ends.
Inputs may be any that keep to these rules, and one draw needn't show every extreme that they name: `sim`: clipped normal values; the row scales differ between draws. `real`: clipped normal values; the row scales differ between draws. pair_real[s, k] lies in the real blocks of the blk indices next to or equal to that of evolved block s, that is from 8 * (s // 8) - 8 to 8 * (s // 8) + 2 * 8 - 1, within the grid; the entries of one row are distinct; pair_real[s, 0] = s; slots k >= pair_count[s] hold valid but unused numbers. `pair_count`: some evolved block has all 16 slots used in every draw.
All inputs are finite; a program needn't handle non-finite values.
Results may differ from the reference program's by a relative error of at most 0.0085.
Values may be sent and summed in bfloat16 or wider, within the bound.
No kernel may reach another device: no remote copies, remote signals or barrier semaphores. Data moves between devices by JAX's collectives and lax.ppermute only.
A program may use at most 128 MiB of HBM per device.

```python
import math
import jax
import jax.numpy as jnp
from jax import lax

F = 512
BLOCK_ROWS = 256
FAN_MAX = 16
ITERS = 3
REAL_DEV = 8
SIM_BLOCKS = 512
ROWS = 131072


def pair_tables(key):
    local = REAL_DEV
    owner = jnp.arange(SIM_BLOCKS, dtype=jnp.int32) // local
    home = jnp.arange(SIM_BLOCKS, dtype=jnp.int32)
    offsets = jnp.arange(3 * local, dtype=jnp.int32)
    candidates = (owner[:, None] - 1) * local + offsets[None, :]
    valid = (candidates >= 0) & (candidates < SIM_BLOCKS)
    hot_real = jax.random.randint(jax.random.fold_in(key, 1), (SIM_BLOCKS,), 0, 4) == 0
    noise = jax.random.randint(jax.random.fold_in(key, 2), (SIM_BLOCKS, 3 * local), 0, 65536)
    safe = jnp.clip(candidates, 0, SIM_BLOCKS - 1)
    rating = noise + jnp.where(hot_real[safe], 131072, 0) + jnp.where(candidates == home[:, None], 1048576, 0)
    rating = jnp.where(valid, rating + 1, 0) * (3 * local) + offsets[None, :]
    order = lax.top_k(rating, FAN_MAX)[1]
    chosen = jnp.take_along_axis(candidates, order, 1)
    hot_sim = jax.random.randint(jax.random.fold_in(key, 3), (SIM_BLOCKS,), 0, 8) == 0
    forced = jnp.arange(SIM_BLOCKS) == jax.random.randint(jax.random.fold_in(key, 4), (), 0, SIM_BLOCKS)
    light = jax.random.randint(jax.random.fold_in(key, 5), (SIM_BLOCKS,), 2, FAN_MAX // 2 + 1)
    counts = jnp.where(hot_sim | forced, FAN_MAX, light)
    return (chosen.astype(jnp.int32), counts.astype(jnp.int32))


def draw_pair_real(key, part):
    return pair_tables(key)[0]


def draw_pair_count(key, part):
    return pair_tables(key)[1]


def draw_sim(key, part):
    key = jax.random.fold_in(key, 11)
    values = jnp.clip(jax.random.normal(key, (ROWS, F), jnp.float32), -6.0, 6.0)
    return values.astype(jnp.bfloat16)


def draw_real(key, part):
    key = jax.random.fold_in(key, 12)
    values = jnp.clip(jax.random.normal(key, (ROWS, F), jnp.float32), -6.0, 6.0)
    return values.astype(jnp.bfloat16)


def setup_inputs(seed: int = 0) -> dict:
    streams_of = jax.random.split(jax.random.key(seed), 5)
    return {
        "sim": draw_sim(jax.random.fold_in(streams_of[4], 71), 0),
        "real": draw_real(jax.random.fold_in(streams_of[4], 71), 0),
        "pair_real": draw_pair_real(jax.random.fold_in(streams_of[4], 71), 0),
        "pair_count": draw_pair_count(jax.random.fold_in(streams_of[4], 71), 0),
    }


EPS = 0.05
NEG = -1.0e30


def reference(sim, real, pair_real, pair_count):
    sim_tiles = sim.reshape(SIM_BLOCKS, BLOCK_ROWS, F)
    real_tiles = real.reshape(SIM_BLOCKS, BLOCK_ROWS, F)
    sim_norm = jnp.sum(jnp.square(sim_tiles.astype(jnp.float32)), -1)
    real_norm = jnp.sum(jnp.square(real_tiles.astype(jnp.float32)), -1)
    active = jnp.arange(FAN_MAX)[None, :] < pair_count[:, None]
    log_rows = math.log(ROWS)

    def make_tiles(inputs):
        rows_x, norm_x, block_ids = inputs
        dots = jnp.einsum("af,kbf->kab", rows_x.astype(jnp.float32), real_tiles[block_ids].astype(jnp.float32))
        return (norm_x[None, :, None] + real_norm[block_ids][:, None, :] - 2.0 * dots) / F

    cost_tiles = lax.map(make_tiles, (sim_tiles, sim_norm, pair_real))

    def row_update(real_pot):
        def one_block(inputs):
            tiles, block_ids, flags = inputs
            scores = jnp.where(flags[:, None, None], (real_pot[block_ids][:, None, :] - tiles) / EPS, NEG)
            highest = jnp.max(scores, axis=(0, 2))
            totals = jnp.sum(jnp.where(flags[:, None, None], jnp.exp(scores - highest[None, :, None]), 0.0), axis=(0, 2))
            return -EPS * (highest + jnp.log(totals)) - EPS * log_rows
        return lax.map(one_block, (cost_tiles, pair_real, active))

    def column_update(sim_pot):
        def peaks(inputs):
            tiles, row_pot, flags = inputs
            scores = jnp.where(flags[:, None, None], (row_pot[None, :, None] - tiles) / EPS, NEG)
            return jnp.max(scores, 1)
        peak_tiles = lax.map(peaks, (cost_tiles, sim_pot, active))
        flat_ids = pair_real.reshape(-1)
        highest = jax.ops.segment_max(peak_tiles.reshape(-1, BLOCK_ROWS), flat_ids, num_segments=SIM_BLOCKS)

        def sums(inputs):
            tiles, row_pot, flags, block_ids = inputs
            scores = jnp.where(flags[:, None, None], (row_pot[None, :, None] - tiles) / EPS, NEG)
            return jnp.sum(jnp.where(flags[:, None, None], jnp.exp(scores - highest[block_ids][:, None, :]), 0.0), 1)
        sum_tiles = lax.map(sums, (cost_tiles, sim_pot, active, pair_real))
        totals = jax.ops.segment_sum(sum_tiles.reshape(-1, BLOCK_ROWS), flat_ids, num_segments=SIM_BLOCKS)
        return -EPS * (highest + jnp.log(totals)) - EPS * log_rows

    real_pot = jnp.zeros((SIM_BLOCKS, BLOCK_ROWS), jnp.float32)
    sim_pot = real_pot
    for sweep in range(ITERS):
        sim_pot = row_update(real_pot)
        real_pot = column_update(sim_pot)

    def pull_block(inputs):
        tiles, rows_x, block_ids, flags, row_pot = inputs
        weights = jnp.exp((row_pot[None, :, None] + real_pot[block_ids][:, None, :] - tiles) / EPS) * ROWS
        weights = jnp.where(flags[:, None, None], weights, 0.0).astype(jnp.bfloat16)
        wide = weights.astype(jnp.float32)
        totals = jnp.sum(wide, axis=(0, 2))
        sums = jnp.einsum("kab,kbf->af", wide, real_tiles[block_ids].astype(jnp.float32))
        return totals[:, None] * rows_x.astype(jnp.float32) - sums

    pull = lax.map(pull_block, (cost_tiles, sim_tiles, pair_real, active, sim_pot))
    return pull.reshape(ROWS, F), sim_pot.reshape(ROWS), real_pot.reshape(ROWS)
```

```python
import functools
import math

import jax
import jax.numpy as jnp
from jax import lax
from jax.experimental import pallas as pl
from jax.experimental.pallas import tpu as pltpu
from jax.sharding import PartitionSpec as P

BLOCK = 256
ITERS = 3
EPS = 0.05
NEG = -1e30
LOG2E = math.log2(math.e)
LANES = 128
MIB = 1024 * 1024


def log_add(a, b):
    high = jnp.maximum(a, b)
    return high + jnp.log2(jnp.exp2(a - high) + jnp.exp2(b - high))


def core_swap(value):
    owners = lax.axis_size("blk")
    return lax.ppermute(value, "blk", [(i, i ^ 1) for i in range(owners)])


def chip_swap(value):
    owners = lax.axis_size("blk")
    return lax.ppermute(value, "blk", [(i, (((i + 1) ^ 1) - 1) % owners) for i in range(owners)])


def rep_shift(value, by):
    count = lax.axis_size("rep")
    return lax.ppermute(value, "rep", [(i, (i + by) % count) for i in range(count)])


def rep_flip(value, mask):
    count = lax.axis_size("rep")
    return lax.ppermute(value, "rep", [(i, i ^ mask) for i in range(count)])


def row_pass(cnt_ref, tab_ref, g_ref, vh_ref, u_ref, log_rows):
    part = 128
    for e in range(2):
        count = cnt_ref[e]
        for c in range(BLOCK // part):
            rows = slice(c * part, (c + 1) * part)

            def scores(k):
                vrow = vh_ref[pl.ds(tab_ref[e, k], 1), :]
                return g_ref[e * 16 + k, rows, :] + vrow

            def peak(k, high):
                t = scores(k)
                return jnp.maximum(high, jnp.maximum(t[:, :LANES], t[:, LANES:]))

            high = lax.fori_loop(0, count, peak, jnp.full((part, LANES), NEG, jnp.float32))
            high = jnp.broadcast_to(jnp.max(high, axis=1, keepdims=True), (part, LANES))

            def total(k, acc):
                t = scores(k)
                return acc + jnp.exp2(t[:, :LANES] - high) + jnp.exp2(t[:, LANES:] - high)

            acc = lax.fori_loop(0, count, total, jnp.zeros((part, LANES), jnp.float32))
            acc = jnp.broadcast_to(jnp.sum(acc, axis=1, keepdims=True), (part, LANES))
            u_ref[e * BLOCK + c * part : e * BLOCK + (c + 1) * part, :] = (
                -(high + jnp.log2(acc)) - log_rows
            )


def column_pass(cnt_ref, tab_ref, g_ref, u_ref, l_ref):
    window = l_ref.shape[0]
    row_ids = lax.broadcasted_iota(jnp.int32, (window, LANES), 0)
    stats = []
    for e in range(2):

        def tile(k, carry):
            here = row_ids == tab_ref[e, k]
            after = []
            for half in range(2):
                lanes = slice(half * LANES, (half + 1) * LANES)
                highs, sums = carry[half]
                t = g_ref[e * 16 + k, :, lanes] + u_ref[e * BLOCK : (e + 1) * BLOCK, :]
                high = jnp.max(t, axis=0, keepdims=True)
                total = jnp.sum(jnp.exp2(t - high), axis=0, keepdims=True)
                after.append((jnp.where(here, high, highs), jnp.where(here, total, sums)))
            return tuple(after)

        start = (jnp.full((window, LANES), NEG, jnp.float32), jnp.ones((window, LANES), jnp.float32))
        found = lax.fori_loop(0, cnt_ref[e], tile, (start, start))
        stats.append([high + jnp.log2(total) for high, total in found])
    for half in range(2):
        l_ref[:, half * LANES : (half + 1) * LANES] = log_add(stats[0][half], stats[1][half])


def build_kernel(
    log_rows, scale, cnt_ref, tab_ref, q_ref, sim_ref, vh_ref, *refs
):
    pieces, (g_ref, win_ref, l_ref), scratch = refs[:12], refs[12:15], refs[15:]
    u_ref, sems = scratch
    rows = pieces[0].shape[0]
    copies = []
    for group in range(3):
        for source in range(4):
            q = pl.multiple_of(q_ref[source] * LANES, LANES)
            i = group * 4 + source
            copies.append(
                pltpu.make_async_copy(
                    pieces[i],
                    win_ref.at[pl.ds(group * rows, rows), pl.ds(q, LANES)],
                    sems.at[i],
                )
            )
    for copy in copies:
        copy.start()
    for copy in copies:
        copy.wait()
    for e in range(2):

        def tile(k, carry):
            w = tab_ref[e, k]
            start = pl.multiple_of(w * BLOCK, BLOCK)
            dots = lax.dot_general(
                sim_ref[e * BLOCK : (e + 1) * BLOCK, :],
                win_ref[pl.ds(start, BLOCK), :],
                (((1,), (1,)), ((), ())),
                preferred_element_type=jnp.float32,
            )
            g_ref[e * 16 + k] = dots * scale
            return carry

        lax.fori_loop(0, cnt_ref[e], tile, 0)
    row_pass(cnt_ref, tab_ref, g_ref, vh_ref, u_ref, log_rows)
    column_pass(cnt_ref, tab_ref, g_ref, u_ref, l_ref)


def sweep_kernel(log_rows, cnt_ref, tab_ref, v0_ref, v1_ref, v2_ref, g_ref, l_ref, u_ref, row_ref, vh_ref):
    local = v0_ref.shape[0]
    vh_ref[0:local, :] = v0_ref[...]
    vh_ref[local : 2 * local, :] = v1_ref[...]
    vh_ref[2 * local : 3 * local, :] = v2_ref[...]
    row_pass(cnt_ref, tab_ref, g_ref, vh_ref, u_ref, log_rows)
    for e in range(2):
        row_ref[e : e + 1, :] = jnp.transpose(u_ref[e * BLOCK : (e + 1) * BLOCK, :])[0:1, :]
    column_pass(cnt_ref, tab_ref, g_ref, u_ref, l_ref)


def pull_kernel(log_rows, cnt_ref, tab_ref, v0_ref, v1_ref, v2_ref, u_ref, sim_ref, g_ref, win_ref, out_ref, vh_ref, tot_ref):
    local = v0_ref.shape[0]
    vh_ref[0:local, :] = v0_ref[...]
    vh_ref[local : 2 * local, :] = v1_ref[...]
    vh_ref[2 * local : 3 * local, :] = v2_ref[...]
    for e in range(2):
        rows = slice(e * BLOCK, (e + 1) * BLOCK)
        out_ref[rows, :] = jnp.zeros((BLOCK, out_ref.shape[1]), jnp.float32)
        tot_ref[...] = jnp.zeros(tot_ref.shape, jnp.float32)

        def tile(k, carry):
            w = tab_ref[e, k]
            vrow = vh_ref[pl.ds(w, 1), :] + log_rows
            u = u_ref[rows, :]
            t = g_ref[e * 16 + k]
            left = jnp.exp2(t[:, :LANES] + u + vrow[:, :LANES]).astype(jnp.bfloat16)
            right = jnp.exp2(t[:, LANES:] + u + vrow[:, LANES:]).astype(jnp.bfloat16)
            tot_ref[...] += left.astype(jnp.float32) + right.astype(jnp.float32)
            start = pl.multiple_of(w * BLOCK, BLOCK)
            out_ref[rows, :] += jnp.dot(
                jnp.concatenate([left, right], axis=1),
                win_ref[pl.ds(start, BLOCK), :],
                preferred_element_type=jnp.float32,
            )
            return carry

        lax.fori_loop(0, cnt_ref[e], tile, 0)
        totals = jnp.sum(tot_ref[...], axis=1, keepdims=True)
        out_ref[rows, :] = totals * sim_ref[rows, :].astype(jnp.float32) - out_ref[rows, :]


def vmem():
    return pl.BlockSpec(memory_space=pltpu.VMEM)


def smem():
    return pl.BlockSpec(memory_space=pltpu.SMEM)


def shards(sim, real, pair_real, pair_count):
    replicas = lax.axis_size("rep")
    owners = lax.axis_size("blk")
    features = sim.shape[1]
    local = real.shape[0] // BLOCK
    rows_total = owners * real.shape[0]
    log_rows = math.log2(rows_total)
    unit = LOG2E / EPS / features
    mine = lax.axis_index("blk")
    rep = lax.axis_index("rep")
    fan = pair_real.shape[1]
    group = pair_real // local - mine
    group = jnp.clip(jnp.where(mine % 2 == 0, group + 1, 1 - group), 0, 2)
    table = group * local + pair_real % local
    quarters = (rep + jnp.array([0, replicas - 1, 1, 2], jnp.int32)) % replicas

    own = real
    from_low = rep_shift(own, 1)
    from_high = rep_shift(own, -1)
    half = own.shape[0] // 2
    far_a = rep_shift(from_low[:half], 1)
    far_b = rep_shift(from_high[half:], -1)
    near = jnp.stack([from_low, from_high])
    far = jnp.concatenate([far_a, far_b])
    pieces = []
    middle = [own, from_low, from_high, far]
    sides = []
    for swap in (chip_swap, core_swap):
        first = swap(own)
        second = swap(near)
        third = swap(far)
        sides.append([first, second[0], second[1], third])
    groups = [sides[0], middle, sides[1]]
    pieces = [piece for parts in groups for piece in parts]
    norms = [
        sum(jnp.sum(jnp.square(p.astype(jnp.float32)), -1) for p in parts).reshape(local, BLOCK) * unit
        for parts in groups
    ]
    sim_norm = jnp.sum(jnp.square(sim.astype(jnp.float32)), -1) * unit

    tiles = 2 * fan
    window = 3 * local
    stats_shape = jax.ShapeDtypeStruct((window, BLOCK), jnp.float32)
    potentials = pltpu.VMEM((2 * BLOCK, LANES), jnp.float32)
    cost, window_rows, stats_out = pl.pallas_call(
        functools.partial(build_kernel, log_rows, 2.0 * unit),
        out_shape=[
            pltpu.VMEM((tiles, BLOCK, BLOCK), jnp.float32),
            pltpu.VMEM((window * BLOCK, features), jnp.bfloat16),
            stats_shape,
        ],
        in_specs=[smem()] * 3 + [vmem()] * 2 + [pl.BlockSpec(memory_space=pl.ANY)] * 12,
        out_specs=[vmem()] * 3,
        scratch_shapes=[potentials, pltpu.SemaphoreType.DMA((12,))],
        compiler_params=pltpu.CompilerParams(vmem_limit_bytes=30 * MIB),
    )(pair_count, table, quarters, sim, -jnp.concatenate(norms), *pieces)

    for sweep in range(ITERS):
        if sweep:
            stats_out, sim_pot, sim_row = pl.pallas_call(
                functools.partial(sweep_kernel, log_rows),
                out_shape=[
                    stats_shape,
                    jax.ShapeDtypeStruct((2 * BLOCK, LANES), jnp.float32),
                    jax.ShapeDtypeStruct((2, BLOCK), jnp.float32),
                ],
                in_specs=[smem()] * 2 + [vmem()] * 4,
                out_specs=[vmem()] * 3,
                scratch_shapes=[pltpu.VMEM((window, BLOCK), jnp.float32)],
                compiler_params=pltpu.CompilerParams(vmem_limit_bytes=30 * MIB),
            )(pair_count, table, *around, pltpu.with_memory_space_constraint(cost, pltpu.VMEM))
        merged = log_add(stats_out, rep_flip(stats_out, 1))
        merged = log_add(merged, rep_flip(merged, 3))
        from_core = core_swap(merged[2 * local :])
        from_chip = chip_swap(merged[:local])
        potential = -log_add(log_add(merged[local : 2 * local], from_core), from_chip) - log_rows
        around = (chip_swap(potential), potential, core_swap(potential))

    pull = pl.pallas_call(
        functools.partial(pull_kernel, log_rows),
        out_shape=jax.ShapeDtypeStruct(sim.shape, jnp.float32),
        in_specs=[smem()] * 2 + [vmem()] * 7,
        out_specs=vmem(),
        scratch_shapes=[
            pltpu.VMEM((window, BLOCK), jnp.float32),
            pltpu.VMEM((BLOCK, LANES), jnp.float32),
        ],
        compiler_params=pltpu.CompilerParams(vmem_limit_bytes=30 * MIB),
    )(
        pair_count,
        table,
        *around,
        sim_pot,
        sim,
        pltpu.with_memory_space_constraint(cost, pltpu.VMEM),
        pltpu.with_memory_space_constraint(window_rows, pltpu.VMEM),
    )
    back = EPS / LOG2E
    sim_out = (sim_row.reshape(-1) + sim_norm) * back
    real_out = ((potential + norms[1]) * back).reshape(-1)
    return (pull, sim_out, real_out)


def solution(mesh):
    in_specs = (
        P(("blk", "rep"), None),
        P("blk", "rep"),
        P(("blk", "rep"), None),
        P(("blk", "rep")),
    )
    out_specs = (P(("blk", "rep"), None), P(("blk", "rep")), P("blk"))
    return jax.shard_map(shards, mesh=mesh, in_specs=in_specs, out_specs=out_specs, check_vma=False)
```

```python
import functools
import math

import jax
import jax.numpy as jnp
from jax import lax
from jax.experimental import pallas as pl
from jax.experimental.pallas import tpu as pltpu
from jax.sharding import PartitionSpec as P

BLOCK = 256
ITERS = 3
EPS = 0.05
NEG = -1e30
LOG2E = math.log2(math.e)
LANES = 128
MIB = 1024 * 1024


def log_add(a, b):
    high = jnp.maximum(a, b)
    return high + jnp.log2(jnp.exp2(a - high) + jnp.exp2(b - high))


def across(index, owners):
    other = ((index + 1) ^ 1) - 1
    return other if 0 <= other < owners else index


def core_swap(value):
    owners = lax.axis_size("blk")
    return lax.ppermute(value, "blk", [(i, i ^ 1) for i in range(owners)])


def chip_swap(value):
    owners = lax.axis_size("blk")
    return lax.ppermute(value, "blk", [(i, across(i, owners)) for i in range(owners)])


def chip_then_core(value):
    owners = lax.axis_size("blk")
    return lax.ppermute(value, "blk", [(i, across(i, owners) ^ 1) for i in range(owners)])


def core_then_chip(value):
    owners = lax.axis_size("blk")
    return lax.ppermute(value, "blk", [(i, across(i ^ 1, owners)) for i in range(owners)])


def rep_shift(value, by):
    count = lax.axis_size("rep")
    return lax.ppermute(value, "rep", [(i, (i + by) % count) for i in range(count)])


def row_pass(cnt_ref, tab_ref, g_ref, vh_ref, u_ref, log_rows, stride=1):
    part = 128
    for e in range(2):
        count = cnt_ref[e]
        for c in range(BLOCK // part):
            rows = slice(c * part, (c + 1) * part)

            def scores(k):
                vrow = vh_ref[pl.ds(tab_ref[e, k] * stride, 1), :]
                return g_ref[e * 16 + k, rows, :] + vrow

            def peak(k, high):
                t = scores(k)
                return jnp.maximum(high, jnp.maximum(t[:, :LANES], t[:, LANES:]))

            high = lax.fori_loop(0, count, peak, jnp.full((part, LANES), NEG, jnp.float32))
            high = jnp.broadcast_to(jnp.max(high, axis=1, keepdims=True), (part, LANES))

            def total(k, acc):
                t = scores(k)
                return acc + jnp.exp2(t[:, :LANES] - high) + jnp.exp2(t[:, LANES:] - high)

            acc = lax.fori_loop(0, count, total, jnp.zeros((part, LANES), jnp.float32))
            acc = jnp.broadcast_to(jnp.sum(acc, axis=1, keepdims=True), (part, LANES))
            u_ref[e * BLOCK + c * part : e * BLOCK + (c + 1) * part, :] = (
                -(high + jnp.log2(acc)) - log_rows
            )


def column_pass(cnt_ref, tab_ref, g_ref, u_ref, l_ref):
    window = l_ref.shape[0]
    row_ids = lax.broadcasted_iota(jnp.int32, (window, LANES), 0)
    stats = []
    for e in range(2):

        def tile(k, carry):
            here = row_ids == tab_ref[e, k]
            after = []
            for half in range(2):
                lanes = slice(half * LANES, (half + 1) * LANES)
                highs, sums = carry[half]
                t = g_ref[e * 16 + k, :, lanes] + u_ref[e * BLOCK : (e + 1) * BLOCK, :]
                high = jnp.max(t, axis=0, keepdims=True)
                total = jnp.sum(jnp.exp2(t - high), axis=0, keepdims=True)
                after.append((jnp.where(here, high, highs), jnp.where(here, total, sums)))
            return tuple(after)

        start = (jnp.full((window, LANES), NEG, jnp.float32), jnp.ones((window, LANES), jnp.float32))
        found = lax.fori_loop(0, cnt_ref[e], tile, (start, start))
        stats.append([high + jnp.log2(total) for high, total in found])
    for half in range(2):
        l_ref[:, half * LANES : (half + 1) * LANES] = log_add(stats[0][half], stats[1][half])


def group_kernel(group, last, log_rows, unit, cnt_ref, tab_ref, q_ref, sim_ref, own_ref, near_ref, far_ref, *refs):
    if group != 1:
        refs = refs[3:]
    g_ref, win_ref, nv_ref = refs[:3]
    refs = refs[3:]
    sems = refs[-1]
    rows = own_ref.shape[0]
    local = rows // BLOCK
    sources = [own_ref, near_ref.at[0], near_ref.at[1], far_ref]
    copies = []
    for i, source in enumerate(sources):
        q = pl.multiple_of(q_ref[i] * LANES, LANES)
        target = win_ref.at[pl.ds(group * rows, rows), pl.ds(q, LANES)]
        copies.append(pltpu.make_async_copy(source, target, sems.at[i]))
    for copy in copies:
        copy.start()
    for copy in copies:
        copy.wait()

    ones = jnp.ones((8, LANES), jnp.bfloat16)

    def norms(i, carry):
        start = pl.multiple_of((group * local + i) * BLOCK, BLOCK)
        y = win_ref[pl.ds(start, BLOCK), :].astype(jnp.float32)
        y = y * y
        part = (y[:, :LANES] + y[:, LANES : 2 * LANES]) + (y[:, 2 * LANES : 3 * LANES] + y[:, 3 * LANES :])
        total = jnp.zeros((8, BLOCK), jnp.float32)
        for _ in range(3):
            piece = part.astype(jnp.bfloat16)
            part = part - piece.astype(jnp.float32)
            total = total + lax.dot_general(
                ones, piece, (((1,), (1,)), ((), ())), preferred_element_type=jnp.float32
            )
        nv_ref[pl.ds(pl.multiple_of((group * local + i) * 8, 8), 8), :] = total * (-unit)
        return carry

    lax.fori_loop(0, local, norms, 0)
    for e in range(2):

        def tile(k, carry):
            w = tab_ref[e, k]

            @pl.when(w // local == group)
            def _():
                start = pl.multiple_of(w * BLOCK, BLOCK)
                dots = lax.dot_general(
                    sim_ref[e * BLOCK : (e + 1) * BLOCK, :],
                    win_ref[pl.ds(start, BLOCK), :],
                    (((1,), (1,)), ((), ())),
                    preferred_element_type=jnp.float32,
                )
                g_ref[e * 16 + k] = dots * (2.0 * unit)

            return carry

        lax.fori_loop(0, cnt_ref[e], tile, 0)
    if last:
        l_ref, u_ref = refs[:2]
        row_pass(cnt_ref, tab_ref, g_ref, nv_ref, u_ref, log_rows, stride=8)
        column_pass(cnt_ref, tab_ref, g_ref, u_ref, l_ref)


def joined(stats_refs, log_rows):
    a, b, c, d = [ref[...] for ref in stats_refs]
    high = jnp.maximum(jnp.maximum(a, b), jnp.maximum(c, d))
    total = jnp.exp2(a - high) + jnp.exp2(b - high) + jnp.exp2(c - high) + jnp.exp2(d - high)
    return -(high + jnp.log2(total)) - log_rows


def sweep_kernel(log_rows, cnt_ref, tab_ref, s0, s1, s2, s3, g_ref, l_ref, u_ref, row_ref, vh_ref):
    vh_ref[...] = joined((s0, s1, s2, s3), log_rows)
    row_pass(cnt_ref, tab_ref, g_ref, vh_ref, u_ref, log_rows)
    for e in range(2):
        row_ref[e : e + 1, :] = jnp.transpose(u_ref[e * BLOCK : (e + 1) * BLOCK, :])[0:1, :]
    column_pass(cnt_ref, tab_ref, g_ref, u_ref, l_ref)


def pull_kernel(
    log_rows, cnt_ref, tab_ref, s0, s1, s2, s3, u_ref, sim_ref, g_ref, win_ref, out_ref, vh_ref, tot_ref
):
    vh_ref[...] = joined((s0, s1, s2, s3), log_rows)
    for e in range(2):
        rows = slice(e * BLOCK, (e + 1) * BLOCK)
        out_ref[rows, :] = jnp.zeros((BLOCK, out_ref.shape[1]), jnp.float32)
        tot_ref[...] = jnp.zeros(tot_ref.shape, jnp.float32)

        def tile(k, carry):
            w = tab_ref[e, k]
            vrow = vh_ref[pl.ds(w, 1), :] + log_rows
            u = u_ref[rows, :]
            t = g_ref[e * 16 + k]
            left = jnp.exp2(t[:, :LANES] + u + vrow[:, :LANES]).astype(jnp.bfloat16)
            right = jnp.exp2(t[:, LANES:] + u + vrow[:, LANES:]).astype(jnp.bfloat16)
            tot_ref[...] += left.astype(jnp.float32) + right.astype(jnp.float32)
            start = pl.multiple_of(w * BLOCK, BLOCK)
            out_ref[rows, :] += jnp.dot(
                jnp.concatenate([left, right], axis=1),
                win_ref[pl.ds(start, BLOCK), :],
                preferred_element_type=jnp.float32,
            )
            return carry

        lax.fori_loop(0, cnt_ref[e], tile, 0)
        totals = jnp.sum(tot_ref[...], axis=1, keepdims=True)
        out_ref[rows, :] = totals * sim_ref[rows, :].astype(jnp.float32) - out_ref[rows, :]


def vmem():
    return pl.BlockSpec(memory_space=pltpu.VMEM)


def smem():
    return pl.BlockSpec(memory_space=pltpu.SMEM)


def shards(sim, real, pair_real, pair_count):
    replicas = lax.axis_size("rep")
    owners = lax.axis_size("blk")
    features = sim.shape[1]
    local = real.shape[0] // BLOCK
    rows_total = owners * real.shape[0]
    log_rows = math.log2(rows_total)
    unit = LOG2E / EPS / features
    mine = lax.axis_index("blk")
    rep = lax.axis_index("rep")
    fan = pair_real.shape[1]
    group = pair_real // local - mine
    group = jnp.clip(jnp.where(mine % 2 == 0, group + 1, 1 - group), 0, 2)
    table = group * local + pair_real % local
    quarters = (rep + jnp.array([0, replicas - 1, 1, 2], jnp.int32)) % replicas

    own = real
    from_low = rep_shift(own, 1)
    from_high = rep_shift(own, -1)
    chip_own = chip_swap(own)
    core_own = core_swap(own)
    from_low, from_high, chip_own = lax.optimization_barrier((from_low, from_high, chip_own))
    half = own.shape[0] // 2
    far = jnp.concatenate([rep_shift(from_low[:half], 1), rep_shift(from_high[half:], -1)])
    near = jnp.stack([from_low, from_high])
    groups = {
        1: (own, near, far),
        2: (core_own, core_swap(near), core_swap(far)),
        0: (chip_own, chip_swap(near), chip_swap(far)),
    }
    sim_norm = jnp.sum(jnp.square(sim.astype(jnp.float32)), -1) * unit

    tiles = 2 * fan
    window = 3 * local
    stats_shape = jax.ShapeDtypeStruct((window, BLOCK), jnp.float32)
    potentials = (2 * BLOCK, LANES)
    held = []
    for group in (1, 2, 0):
        last = group == 0
        found = pl.pallas_call(
            functools.partial(group_kernel, group, last, log_rows, unit),
            out_shape=[
                pltpu.VMEM((tiles, BLOCK, BLOCK), jnp.float32),
                pltpu.VMEM((window * BLOCK, features), jnp.bfloat16),
                jax.ShapeDtypeStruct((window * 8, BLOCK), jnp.float32),
            ]
            + [stats_shape] * last,
            in_specs=[smem()] * 3 + [vmem()] + [pl.BlockSpec(memory_space=pl.ANY)] * 3 + [vmem()] * len(held),
            out_specs=[vmem()] * (3 + last),
            input_output_aliases={7 + i: i for i in range(len(held))},
            scratch_shapes=[pltpu.VMEM(potentials, jnp.float32)] * last + [pltpu.SemaphoreType.DMA((4,))],
            compiler_params=pltpu.CompilerParams(vmem_limit_bytes=24 * MIB),
            cost_estimate=pl.CostEstimate(flops=10**9, bytes_accessed=8 * MIB, transcendentals=0),
        )(pair_count, table, quarters, sim, *groups[group], *held)
        held = [pltpu.with_memory_space_constraint(value, pltpu.VMEM) for value in found[:2]] + [found[2]]
    cost, window_rows, norms = held
    stats_out = found[3]

    for sweep in range(ITERS):
        if sweep:
            stats_out, sim_pot, sim_row = pl.pallas_call(
                functools.partial(sweep_kernel, log_rows),
                out_shape=[
                    stats_shape,
                    jax.ShapeDtypeStruct(potentials, jnp.float32),
                    jax.ShapeDtypeStruct((2, BLOCK), jnp.float32),
                ],
                in_specs=[smem()] * 2 + [vmem()] * 5,
                out_specs=[vmem()] * 3,
                scratch_shapes=[pltpu.VMEM((window, BLOCK), jnp.float32)],
                compiler_params=pltpu.CompilerParams(vmem_limit_bytes=24 * MIB),
            )(pair_count, table, *around, cost)
        core = core_swap(stats_out[local:])
        chip = chip_swap(stats_out[: 2 * local])
        past_core = chip_then_core(stats_out[:local])
        past_chip = core_then_chip(stats_out[2 * local :])
        merged = jnp.concatenate(
            [
                log_add(stats_out[:local], log_add(chip[local:], past_chip)),
                log_add(stats_out[local : 2 * local], log_add(chip[:local], core[local:])),
                log_add(stats_out[2 * local :], log_add(core[:local], past_core)),
            ]
        )
        around = (merged, rep_shift(merged, 1), rep_shift(merged, -1), rep_shift(merged, 2))

    pull, potential = pl.pallas_call(
        functools.partial(pull_kernel, log_rows),
        out_shape=[
            jax.ShapeDtypeStruct(sim.shape, jnp.float32),
            jax.ShapeDtypeStruct((window, BLOCK), jnp.float32),
        ],
        in_specs=[smem()] * 2 + [vmem()] * 8,
        out_specs=[vmem()] * 2,
        scratch_shapes=[pltpu.VMEM((BLOCK, LANES), jnp.float32)],
        compiler_params=pltpu.CompilerParams(vmem_limit_bytes=30 * MIB),
    )(
        pair_count,
        table,
        *around,
        sim_pot,
        sim,
        cost,
        window_rows,
    )
    back = EPS / LOG2E
    sim_out = (sim_row.reshape(-1) + sim_norm) * back
    own_rows = norms.reshape(window, 8, BLOCK)[local : 2 * local, 0]
    real_out = ((potential[local : 2 * local] - own_rows) * back).reshape(-1)
    return (pull, sim_out, real_out)


def solution(mesh):
    in_specs = (
        P(("blk", "rep"), None),
        P("blk", "rep"),
        P(("blk", "rep"), None),
        P(("blk", "rep")),
    )
    out_specs = (P(("blk", "rep"), None), P(("blk", "rep")), P("blk"))
    return jax.shard_map(shards, mesh=mesh, in_specs=in_specs, out_specs=out_specs, check_vma=False)
```

```python
import functools
import math

import jax
import jax.numpy as jnp
from jax import lax
from jax.experimental import pallas as pl
from jax.experimental.pallas import tpu as pltpu
from jax.sharding import PartitionSpec as P

BLOCK = 256
ITERS = 3
EPS = 0.05
NEG = -1e30
LOG2E = math.log2(math.e)
LANES = 128
FAN = 16
LEAST, MOST = 2.0**-40, 2.0**40
HALF_NEG = -5e29
MIB = 1024 * 1024


def log_add(a, b):
    high = jnp.maximum(a, b)
    return high + jnp.log2(jnp.exp2(a - high) + jnp.exp2(b - high))


def across(index, owners):
    other = ((index + 1) ^ 1) - 1
    return other if 0 <= other < owners else index


def core_swap(value):
    owners = lax.axis_size("blk")
    return lax.ppermute(value, "blk", [(i, i ^ 1) for i in range(owners)])


def chip_swap(value):
    owners = lax.axis_size("blk")
    return lax.ppermute(value, "blk", [(i, across(i, owners)) for i in range(owners)])


def chip_then_core(value):
    owners = lax.axis_size("blk")
    return lax.ppermute(value, "blk", [(i, across(i, owners) ^ 1) for i in range(owners)])


def core_then_chip(value):
    owners = lax.axis_size("blk")
    return lax.ppermute(value, "blk", [(i, across(i ^ 1, owners)) for i in range(owners)])


def rep_shift(value, by):
    count = lax.axis_size("rep")
    return lax.ppermute(value, "rep", [(i, (i + by) % count) for i in range(count)])


def row_pass(cnt_ref, tab_ref, t_ref, v_ref, m_ref, u_ref, log_rows):
    part = 128
    for e in range(2):
        count = cnt_ref[e]
        for c in range(BLOCK // part):
            rows = slice(c * part, (c + 1) * part)

            def scores(k):
                return t_ref[e * 16 + k, rows, :] + v_ref[pl.ds(tab_ref[e, k], 1), :]

            def peak(k, high):
                t = scores(k)
                return jnp.maximum(high, jnp.maximum(t[:, :LANES], t[:, LANES:]))

            high = lax.fori_loop(0, count, peak, jnp.full((part, LANES), NEG, jnp.float32))
            high = jnp.broadcast_to(jnp.max(high, axis=1, keepdims=True), (part, LANES))

            def total(k, acc):
                t = scores(k)
                return acc + jnp.exp2(t[:, :LANES] - high) + jnp.exp2(t[:, LANES:] - high)

            acc = lax.fori_loop(0, count, total, jnp.zeros((part, LANES), jnp.float32))
            acc = jnp.broadcast_to(jnp.sum(acc, axis=1, keepdims=True), (part, LANES))
            u_ref[e * BLOCK + c * part : e * BLOCK + (c + 1) * part, :] = (
                -(high + jnp.log2(acc)) - log_rows
            )


def column_pass(cnt_ref, tab_ref, t_ref, u_ref, l_ref):
    window = l_ref.shape[0]
    row_ids = lax.broadcasted_iota(jnp.int32, (window, LANES), 0)
    stats = []
    for e in range(2):

        def tile(k, carry):
            here = row_ids == tab_ref[e, k]
            after = []
            for half in range(2):
                lanes = slice(half * LANES, (half + 1) * LANES)
                highs, sums = carry[half]
                t = t_ref[e * 16 + k, :, lanes] + u_ref[e * BLOCK : (e + 1) * BLOCK, :]
                high = jnp.max(t, axis=0, keepdims=True)
                total = jnp.sum(jnp.exp2(t - high), axis=0, keepdims=True)
                after.append((jnp.where(here, high, highs), jnp.where(here, total, sums)))
            return tuple(after)

        start = (jnp.full((window, LANES), NEG, jnp.float32), jnp.ones((window, LANES), jnp.float32))
        found = lax.fori_loop(0, cnt_ref[e], tile, (start, start))
        stats.append([high + jnp.log2(total) for high, total in found])
    for half in range(2):
        l_ref[:, half * LANES : (half + 1) * LANES] = log_add(stats[0][half], stats[1][half])


def lanes_of(column, rows):
    return jnp.broadcast_to(column, (rows, LANES))


def scaled_columns(cnt_ref, tab_ref, p_ref, a_ref, c_ref):
    c_ref[...] = jnp.zeros(c_ref.shape, jnp.float32)
    for e in range(2):

        def tile(k, carry):
            a = a_ref[e * BLOCK : (e + 1) * BLOCK, :]
            p = p_ref[e * 16 + k]
            at = pl.ds(pl.multiple_of(tab_ref[e, k] * 8, 8), 8)
            for half in range(2):
                lanes = slice(half * LANES, (half + 1) * LANES)
                terms = (p[:, lanes] * a).reshape(BLOCK // 8, 8, LANES)
                c_ref[at, lanes] += jnp.sum(terms, axis=0)
            return carry

        lax.fori_loop(0, cnt_ref[e], tile, 0)
    window = c_ref.shape[0] // 8
    return jnp.sum(c_ref[...].reshape(window, 8, BLOCK), axis=1)


def scaled_rows(cnt_ref, tab_ref, p_ref, b_ref, r_ref):
    for e in range(2):

        def tile(k, acc):
            p = p_ref[e * 16 + k]
            b = b_ref[pl.ds(tab_ref[e, k], 1), :]
            return acc + p[:, :LANES] * b[:, :LANES] + p[:, LANES:] * b[:, LANES:]

        acc = lax.fori_loop(0, cnt_ref[e], tile, jnp.zeros((BLOCK, LANES), jnp.float32))
        r_ref[e * BLOCK : (e + 1) * BLOCK, :] = lanes_of(jnp.sum(acc, axis=1, keepdims=True), BLOCK)


def within(value):
    return jnp.logical_and(jnp.min(value) >= LEAST, jnp.max(value) <= MOST)


def columns_out(cnt_ref, tab_ref, t_ref, p_ref, a_ref, u_ref, used_ref, c_ref, l_ref, log_rows, good):
    used = used_ref[...] > 0.0
    total = jnp.where(used, scaled_columns(cnt_ref, tab_ref, p_ref, a_ref, c_ref), 1.0)
    good = jnp.logical_and(good, within(total))
    l_ref[...] = jnp.where(used, jnp.log2(total) - log_rows, NEG)

    @pl.when(jnp.logical_not(good))
    def _():
        column_pass(cnt_ref, tab_ref, t_ref, u_ref, l_ref)


def group_kernel(group, log_rows, unit, cnt_ref, tab_ref, order_ref, bounds_ref, q_ref, sim_ref, own_ref, near_ref, far_ref, *refs):
    last = group == 0
    if last:
        used_ref, refs = refs[0], refs[1:]
    if group != 1:
        refs = refs[3:]
    t_ref, win_ref, m_ref = refs[:3]
    refs = refs[3:]
    n_ref, sems = refs[-2:]
    rows = own_ref.shape[0]
    local = rows // BLOCK
    sources = [own_ref, near_ref.at[0], near_ref.at[1], far_ref]
    copies = []
    for i, source in enumerate(sources):
        q = pl.multiple_of(q_ref[i] * LANES, LANES)
        target = win_ref.at[pl.ds(group * rows, rows), pl.ds(q, LANES)]
        copies.append(pltpu.make_async_copy(source, target, sems.at[i]))
    for copy in copies:
        copy.start()
    if group == 1:
        m_ref[...] = jnp.full(m_ref.shape, NEG, jnp.float32)
    for copy in copies:
        copy.wait()

    ones = jnp.ones((8, LANES), jnp.bfloat16)

    def norms(i, carry):
        start = pl.multiple_of((group * local + i) * BLOCK, BLOCK)
        y = win_ref[pl.ds(start, BLOCK), :].astype(jnp.float32)
        y = y * y
        part = (y[:, :LANES] + y[:, LANES : 2 * LANES]) + (y[:, 2 * LANES : 3 * LANES] + y[:, 3 * LANES :])
        total = jnp.zeros((8, BLOCK), jnp.float32)
        for _ in range(3):
            piece = part.astype(jnp.bfloat16)
            part = part - piece.astype(jnp.float32)
            total = total + lax.dot_general(
                ones, piece, (((1,), (1,)), ((), ())), preferred_element_type=jnp.float32
            )
        n_ref[pl.ds(pl.multiple_of(i * 8, 8), 8), :] = total * unit
        return carry

    lax.fori_loop(0, local, norms, 0, unroll=4)
    first, end = bounds_ref[group], bounds_ref[group + 1]

    def build(slot):
        e = slot // FAN
        w = tab_ref[e, slot % FAN]
        block = pl.ds(pl.multiple_of(e * BLOCK, BLOCK), BLOCK)
        start = pl.multiple_of(w * BLOCK, BLOCK)
        dots = lax.dot_general(
            sim_ref[block, :],
            win_ref[pl.ds(start, BLOCK), :],
            (((1,), (1,)), ((), ())),
            preferred_element_type=jnp.float32,
        )
        t = dots * (2.0 * unit) - n_ref[pl.ds((w % local) * 8, 1), :]
        t_ref[slot] = t
        m_ref[block, :] = jnp.maximum(m_ref[block, :], jnp.maximum(t[:, :LANES], t[:, LANES:]))

    def pair(i, carry):
        at = first + 2 * i
        build(order_ref[at])
        build(order_ref[jnp.minimum(at + 1, end - 1)])
        return carry

    lax.fori_loop(0, (end - first + 1) // 2, pair, 0)
    if last:
        l_ref, p_ref, u_ref, a_ref, c_ref = refs[:5]
        for e in range(2):
            block = slice(e * BLOCK, (e + 1) * BLOCK)
            high = lanes_of(jnp.max(m_ref[block, :], axis=1, keepdims=True), BLOCK)
            m_ref[block, :] = high

            def plan(k, acc):
                t = t_ref[e * 16 + k]
                high = m_ref[block, :]
                left = jnp.exp2(t[:, :LANES] - high)
                right = jnp.exp2(t[:, LANES:] - high)
                p_ref[e * 16 + k, :, :LANES] = left
                p_ref[e * 16 + k, :, LANES:] = right
                return acc + left + right

            acc = lax.fori_loop(0, cnt_ref[e], plan, jnp.zeros((BLOCK, LANES), jnp.float32))
            acc = lanes_of(jnp.sum(acc, axis=1, keepdims=True), BLOCK)
            a_ref[block, :] = 1.0 / acc
            u_ref[block, :] = -(high + jnp.log2(acc)) - log_rows
        columns_out(cnt_ref, tab_ref, t_ref, p_ref, a_ref, u_ref, used_ref, c_ref, l_ref, log_rows, True)


def joined(stats_refs, log_rows):
    a, b, c, d = [ref[...] for ref in stats_refs]
    high = jnp.maximum(jnp.maximum(a, b), jnp.maximum(c, d))
    total = jnp.exp2(a - high) + jnp.exp2(b - high) + jnp.exp2(c - high) + jnp.exp2(d - high)
    return jnp.where(high > HALF_NEG, -(high + jnp.log2(total)) - log_rows, 0.0)


def sweep_kernel(
    log_rows, cnt_ref, tab_ref, s0, s1, s2, s3, used_ref, m_ref, t_ref, p_ref,
    l_ref, u_ref, row_ref, v_ref, b_ref, a_ref, c_ref
):
    used = used_ref[...] > 0.0
    v = jnp.where(used, joined((s0, s1, s2, s3), log_rows), 0.0)
    v_ref[...] = v
    b = jnp.exp2(v)
    b_ref[...] = b
    scaled_rows(cnt_ref, tab_ref, p_ref, b_ref, a_ref)
    totals = a_ref[...]
    good = jnp.logical_and(within(b), within(totals))
    u_ref[...] = -(m_ref[...] + jnp.log2(totals)) - log_rows
    a_ref[...] = 1.0 / totals

    @pl.when(jnp.logical_not(good))
    def _():
        row_pass(cnt_ref, tab_ref, t_ref, v_ref, m_ref, u_ref, log_rows)

    for e in range(2):
        row_ref[e : e + 1, :] = jnp.transpose(u_ref[e * BLOCK : (e + 1) * BLOCK, :])[0:1, :]
    columns_out(cnt_ref, tab_ref, t_ref, p_ref, a_ref, u_ref, used_ref, c_ref, l_ref, log_rows, good)


def pull_kernel(
    log_rows, cnt_ref, tab_ref, s0, s1, s2, s3, used_ref, m_ref, t_ref, p_ref, u_ref, sim_ref, win_ref,
    out_ref, v_ref, b_ref, a_ref, tot_ref
):
    potential = joined((s0, s1, s2, s3), log_rows)
    v_ref[...] = potential
    v = jnp.where(used_ref[...] > 0.0, potential, 0.0)
    b = jnp.exp2(v)
    b_ref[...] = b
    a = jnp.exp2(u_ref[...] + m_ref[...] + log_rows)
    a_ref[...] = a
    good = jnp.logical_and(within(b), within(a))

    def gather(weights):
        for e in range(2):
            rows = slice(e * BLOCK, (e + 1) * BLOCK)
            out_ref[rows, :] = jnp.zeros((BLOCK, out_ref.shape[1]), jnp.float32)
            tot_ref[...] = jnp.zeros(tot_ref.shape, jnp.float32)

            def pair(i, carry):
                sides, reals = [], []
                sums = tot_ref[...]
                for k in (2 * i, 2 * i + 1):
                    w = tab_ref[e, k]
                    for value in weights(e, k, w, rows):
                        value = jnp.where(k < cnt_ref[e], value, 0.0).astype(jnp.bfloat16)
                        sums += value.astype(jnp.float32)
                        sides.append(value)
                    reals.append(win_ref[pl.ds(pl.multiple_of(w * BLOCK, BLOCK), BLOCK), :])
                tot_ref[...] = sums
                out_ref[rows, :] += jnp.dot(
                    jnp.concatenate(sides, axis=1),
                    jnp.concatenate(reals, axis=0),
                    preferred_element_type=jnp.float32,
                )
                return carry

            lax.fori_loop(0, (cnt_ref[e] + 1) // 2, pair, 0)
            totals = jnp.sum(tot_ref[...], axis=1, keepdims=True)
            out_ref[rows, :] = totals * sim_ref[rows, :].astype(jnp.float32) - out_ref[rows, :]

    def scaled(e, k, w, rows):
        p = p_ref[e * 16 + k]
        b = b_ref[pl.ds(w, 1), :]
        a = a_ref[rows, :]
        return p[:, :LANES] * a * b[:, :LANES], p[:, LANES:] * a * b[:, LANES:]

    def logarithmic(e, k, w, rows):
        t = t_ref[e * 16 + k]
        v = v_ref[pl.ds(w, 1), :] + log_rows
        u = u_ref[rows, :]
        return jnp.exp2(t[:, :LANES] + u + v[:, :LANES]), jnp.exp2(t[:, LANES:] + u + v[:, LANES:])

    @pl.when(good)
    def _():
        gather(scaled)

    @pl.when(jnp.logical_not(good))
    def _():
        gather(logarithmic)


def vmem():
    return pl.BlockSpec(memory_space=pltpu.VMEM)


def smem():
    return pl.BlockSpec(memory_space=pltpu.SMEM)


def shards(sim, real, pair_real, pair_count):
    replicas = lax.axis_size("rep")
    owners = lax.axis_size("blk")
    features = sim.shape[1]
    local = real.shape[0] // BLOCK
    rows_total = owners * real.shape[0]
    log_rows = math.log2(rows_total)
    unit = LOG2E / EPS / features
    mine = lax.axis_index("blk")
    rep = lax.axis_index("rep")
    fan = pair_real.shape[1]
    group = pair_real // local - mine
    group = jnp.clip(jnp.where(mine % 2 == 0, group + 1, 1 - group), 0, 2)
    table = group * local + pair_real % local
    quarters = (rep + jnp.array([0, replicas - 1, 1, 2], jnp.int32)) % replicas

    own = real
    from_low = rep_shift(own, 1)
    from_high = rep_shift(own, -1)
    chip_own = chip_swap(own)
    core_own = core_swap(own)
    from_low, from_high, chip_own = lax.optimization_barrier((from_low, from_high, chip_own))
    half = own.shape[0] // 2
    far = jnp.concatenate([rep_shift(from_low[:half], 1), rep_shift(from_high[half:], -1)])
    near = jnp.stack([from_low, from_high])
    groups = {
        1: (own, near, far),
        2: (core_own, core_swap(near), core_swap(far)),
        0: (chip_own, chip_swap(near), chip_swap(far)),
    }
    sim_norm = jnp.sum(jnp.square(sim.astype(jnp.float32)), -1) * unit

    tiles = 2 * fan
    window = 3 * local
    stats_shape = jax.ShapeDtypeStruct((window, BLOCK), jnp.float32)
    potentials = (2 * BLOCK, LANES)
    active = jnp.arange(fan)[None, :] < pair_count[:, None]
    ids = jnp.arange(tiles, dtype=jnp.int32)
    place = jnp.where(active, table // local, 3).reshape(-1)
    rank = jnp.sum((place * tiles + ids)[None, :] < (place * tiles + ids)[:, None], 1)
    order = jnp.sum(jnp.where(rank[:, None] == ids[None, :], ids[:, None], 0), 0)
    bounds = jnp.sum(place[:, None] < jnp.arange(4)[None, :], 0).astype(jnp.int32)
    hits = (table[:, :, None] == jnp.arange(window)) & active[:, :, None]
    used = jnp.broadcast_to(jnp.any(hits, (0, 1))[:, None], (window, BLOCK)).astype(jnp.float32)
    column = jax.ShapeDtypeStruct(potentials, jnp.float32)
    held = []
    for group in (1, 2, 0):
        last = group == 0
        found = pl.pallas_call(
            functools.partial(group_kernel, group, log_rows, unit),
            out_shape=[
                pltpu.VMEM((tiles, BLOCK, BLOCK), jnp.float32),
                pltpu.VMEM((window * BLOCK, features), jnp.bfloat16),
                column,
            ]
            + [stats_shape, pltpu.VMEM((tiles, BLOCK, BLOCK), jnp.float32)] * last,
            in_specs=[smem()] * 5
            + [vmem()]
            + [pl.BlockSpec(memory_space=pl.ANY)] * 3
            + [vmem()] * (last + len(held)),
            out_specs=[vmem()] * (3 + 2 * last),
            input_output_aliases={9 + last + i: i for i in range(len(held))},
            scratch_shapes=[
                pltpu.VMEM(potentials, jnp.float32),
                pltpu.VMEM(potentials, jnp.float32),
                pltpu.VMEM((window * 8, BLOCK), jnp.float32),
            ]
            * last
            + [pltpu.VMEM((local * 8, BLOCK), jnp.float32), pltpu.SemaphoreType.DMA((4,))],
            compiler_params=pltpu.CompilerParams(vmem_limit_bytes=20 * MIB),
            cost_estimate=pl.CostEstimate(flops=10**9, bytes_accessed=8 * MIB, transcendentals=0),
        )(pair_count, table, order, bounds, quarters, sim, *groups[group], *[used] * last, *held)
        held = [pltpu.with_memory_space_constraint(value, pltpu.VMEM) for value in found[:2]] + [found[2]]
    scores, window_rows, peaks = held
    stats_out = found[3]
    plan = pltpu.with_memory_space_constraint(found[4], pltpu.VMEM)

    for sweep in range(ITERS):
        if sweep:
            stats_out, sim_pot, sim_row = pl.pallas_call(
                functools.partial(sweep_kernel, log_rows),
                out_shape=[stats_shape, column, jax.ShapeDtypeStruct((2, BLOCK), jnp.float32)],
                in_specs=[smem()] * 2 + [vmem()] * 8,
                out_specs=[vmem()] * 3,
                scratch_shapes=[
                    pltpu.VMEM((window, BLOCK), jnp.float32),
                    pltpu.VMEM((window, BLOCK), jnp.float32),
                    pltpu.VMEM(potentials, jnp.float32),
                    pltpu.VMEM((window * 8, BLOCK), jnp.float32),
                ],
                compiler_params=pltpu.CompilerParams(vmem_limit_bytes=20 * MIB),
            )(pair_count, table, *around, used, peaks, scores, plan)
        core = core_swap(stats_out[local:])
        chip = chip_swap(stats_out[: 2 * local])
        past_core = chip_then_core(stats_out[:local])
        past_chip = core_then_chip(stats_out[2 * local :])
        merged = jnp.concatenate(
            [
                log_add(stats_out[:local], log_add(chip[local:], past_chip)),
                log_add(stats_out[local : 2 * local], log_add(chip[:local], core[local:])),
                log_add(stats_out[2 * local :], log_add(core[:local], past_core)),
            ]
        )
        around = (merged, rep_shift(merged, 1), rep_shift(merged, -1), rep_shift(merged, 2))

    pull, potential = pl.pallas_call(
        functools.partial(pull_kernel, log_rows),
        out_shape=[jax.ShapeDtypeStruct(sim.shape, jnp.float32), stats_shape],
        in_specs=[smem()] * 2 + [vmem()] * 11,
        out_specs=[vmem()] * 2,
        scratch_shapes=[
            pltpu.VMEM((window, BLOCK), jnp.float32),
            pltpu.VMEM(potentials, jnp.float32),
            pltpu.VMEM((BLOCK, LANES), jnp.float32),
        ],
        compiler_params=pltpu.CompilerParams(vmem_limit_bytes=20 * MIB),
    )(pair_count, table, *around, used, peaks, scores, plan, sim_pot, sim, window_rows)
    back = EPS / LOG2E
    sim_out = (sim_row.reshape(-1) + sim_norm) * back
    real_out = (potential[local : 2 * local] * back).reshape(-1)
    return (pull, sim_out, real_out)


def solution(mesh):
    in_specs = (
        P(("blk", "rep"), None),
        P("blk", "rep"),
        P(("blk", "rep"), None),
        P(("blk", "rep")),
    )
    out_specs = (P(("blk", "rep"), None), P(("blk", "rep")), P("blk"))
    return jax.shard_map(shards, mesh=mesh, in_specs=in_specs, out_specs=out_specs, check_vma=False)
```

```python
import functools
import math

import jax
import jax.numpy as jnp
from jax import lax
from jax.experimental import pallas as pl
from jax.experimental.pallas import tpu as pltpu
from jax.sharding import PartitionSpec as P

BLOCK = 256
ITERS = 3
EPS = 0.05
NEG = -1e30
LOG2E = math.log2(math.e)
LANES = 128
FAN = 16
LEAST, MOST = 2.0**-40, 2.0**40
HALF_NEG = -5e29
MIB = 1024 * 1024


def log_add(a, b):
    high = jnp.maximum(a, b)
    return high + jnp.log2(jnp.exp2(a - high) + jnp.exp2(b - high))


def across(index, owners):
    other = ((index + 1) ^ 1) - 1
    return other if 0 <= other < owners else index


def core_swap(value):
    owners = lax.axis_size("blk")
    return lax.ppermute(value, "blk", [(i, i ^ 1) for i in range(owners)])


def chip_swap(value):
    owners = lax.axis_size("blk")
    return lax.ppermute(value, "blk", [(i, across(i, owners)) for i in range(owners)])


def chip_then_core(value):
    owners = lax.axis_size("blk")
    return lax.ppermute(value, "blk", [(i, across(i, owners) ^ 1) for i in range(owners)])


def core_then_chip(value):
    owners = lax.axis_size("blk")
    return lax.ppermute(value, "blk", [(i, across(i ^ 1, owners)) for i in range(owners)])


def rep_shift(value, by):
    count = lax.axis_size("rep")
    return lax.ppermute(value, "rep", [(i, (i + by) % count) for i in range(count)])


def row_pass(tab_ref, size_ref, t_ref, v_ref, m_ref, u_ref, log_rows):
    part = 128
    for e in range(2):
        count = size_ref[8 + e]
        for c in range(BLOCK // part):
            rows = slice(c * part, (c + 1) * part)

            def scores(k):
                return t_ref[e * 16 + k, rows, :] + v_ref[pl.ds(tab_ref[e, k], 1), :]

            def peak(k, high):
                t = scores(k)
                return jnp.maximum(high, jnp.maximum(t[:, :LANES], t[:, LANES:]))

            high = lax.fori_loop(0, count, peak, jnp.full((part, LANES), NEG, jnp.float32))
            high = jnp.broadcast_to(jnp.max(high, axis=1, keepdims=True), (part, LANES))

            def total(k, acc):
                t = scores(k)
                return acc + jnp.exp2(t[:, :LANES] - high) + jnp.exp2(t[:, LANES:] - high)

            acc = lax.fori_loop(0, count, total, jnp.zeros((part, LANES), jnp.float32))
            acc = jnp.broadcast_to(jnp.sum(acc, axis=1, keepdims=True), (part, LANES))
            u_ref[e * BLOCK + c * part : e * BLOCK + (c + 1) * part, :] = (
                -(high + jnp.log2(acc)) - log_rows
            )


def column_pass(tab_ref, size_ref, t_ref, u_ref, l_ref):
    window = l_ref.shape[0]
    row_ids = lax.broadcasted_iota(jnp.int32, (window, LANES), 0)
    stats = []
    for e in range(2):

        def tile(k, carry):
            here = row_ids == tab_ref[e, k]
            after = []
            for half in range(2):
                lanes = slice(half * LANES, (half + 1) * LANES)
                highs, sums = carry[half]
                t = t_ref[e * 16 + k, :, lanes] + u_ref[e * BLOCK : (e + 1) * BLOCK, :]
                high = jnp.max(t, axis=0, keepdims=True)
                total = jnp.sum(jnp.exp2(t - high), axis=0, keepdims=True)
                after.append((jnp.where(here, high, highs), jnp.where(here, total, sums)))
            return tuple(after)

        start = (jnp.full((window, LANES), NEG, jnp.float32), jnp.ones((window, LANES), jnp.float32))
        found = lax.fori_loop(0, size_ref[8 + e], tile, (start, start))
        stats.append([high + jnp.log2(total) for high, total in found])
    for half in range(2):
        l_ref[:, half * LANES : (half + 1) * LANES] = log_add(stats[0][half], stats[1][half])


def lanes_of(column, rows):
    return jnp.broadcast_to(column, (rows, LANES))


def scaled_columns(tab_ref, size_ref, p_ref, a_ref, c_ref):
    c_ref[...] = jnp.zeros(c_ref.shape, jnp.float32)
    for e in range(2):

        def tile(k, carry):
            a = a_ref[e * BLOCK : (e + 1) * BLOCK, :]
            p = p_ref[e * 16 + k]
            at = pl.ds(pl.multiple_of(tab_ref[e, k] * 8, 8), 8)
            for half in range(2):
                lanes = slice(half * LANES, (half + 1) * LANES)
                terms = (p[:, lanes] * a).reshape(BLOCK // 8, 8, LANES)
                c_ref[at, lanes] += jnp.sum(terms, axis=0)
            return carry

        lax.fori_loop(0, size_ref[8 + e], tile, 0)
    window = c_ref.shape[0] // 8
    return jnp.sum(c_ref[...].reshape(window, 8, BLOCK), axis=1)


def scaled_rows(tab_ref, size_ref, p_ref, b_ref, r_ref):
    for e in range(2):

        def tile(k, acc):
            p = p_ref[e * 16 + k]
            b = b_ref[pl.ds(tab_ref[e, k], 1), :]
            return acc + p[:, :LANES] * b[:, :LANES] + p[:, LANES:] * b[:, LANES:]

        acc = lax.fori_loop(0, size_ref[8 + e], tile, jnp.zeros((BLOCK, LANES), jnp.float32))
        r_ref[e * BLOCK : (e + 1) * BLOCK, :] = lanes_of(jnp.sum(acc, axis=1, keepdims=True), BLOCK)


def within(value):
    return jnp.logical_and(jnp.min(value) >= LEAST, jnp.max(value) <= MOST)


def columns_out(tab_ref, size_ref, t_ref, p_ref, a_ref, u_ref, used_ref, c_ref, l_ref, log_rows, good):
    used = used_ref[...] > 0.0
    total = jnp.where(used, scaled_columns(tab_ref, size_ref, p_ref, a_ref, c_ref), 1.0)
    good = jnp.logical_and(good, within(total))
    l_ref[...] = jnp.where(used, jnp.log2(total) - log_rows, NEG)

    @pl.when(jnp.logical_not(good))
    def _():
        column_pass(tab_ref, size_ref, t_ref, u_ref, l_ref)


def group_kernel(group, log_rows, unit, tab_ref, order_ref, size_ref, sim_hbm, own_ref, near_ref, far_ref, *refs):
    last = group == 0
    if last:
        used_ref, refs = refs[0], refs[1:]
    if group != 1:
        refs = refs[3:]
    t_ref, win_ref, m_ref = refs[:3]
    refs = refs[3:]
    n_ref, sim_ref, sems = refs[-3:]
    rows = own_ref.shape[0]
    local = rows // BLOCK
    sources = [own_ref, near_ref.at[0], near_ref.at[1], far_ref]
    copies = [pltpu.make_async_copy(sim_hbm, sim_ref, sems.at[4])]
    for i, source in enumerate(sources):
        q = pl.multiple_of(size_ref[4 + i] * LANES, LANES)
        target = win_ref.at[pl.ds(group * rows, rows), pl.ds(q, LANES)]
        copies.append(pltpu.make_async_copy(source, target, sems.at[i]))
    for copy in copies:
        copy.start()
    if group == 1:
        m_ref[...] = jnp.full(m_ref.shape, NEG, jnp.float32)
    for copy in copies:
        copy.wait()

    ones = jnp.ones((8, LANES), jnp.bfloat16)

    def norms(i, carry):
        start = pl.multiple_of((group * local + i) * BLOCK, BLOCK)
        y = win_ref[pl.ds(start, BLOCK), :].astype(jnp.float32)
        y = y * y
        part = (y[:, :LANES] + y[:, LANES : 2 * LANES]) + (y[:, 2 * LANES : 3 * LANES] + y[:, 3 * LANES :])
        total = jnp.zeros((8, BLOCK), jnp.float32)
        for _ in range(3):
            piece = part.astype(jnp.bfloat16)
            part = part - piece.astype(jnp.float32)
            total = total + lax.dot_general(
                ones, piece, (((1,), (1,)), ((), ())), preferred_element_type=jnp.float32
            )
        n_ref[pl.ds(pl.multiple_of(i * 8, 8), 8), :] = total * unit
        return carry

    lax.fori_loop(0, local, norms, 0, unroll=4)
    first, end = size_ref[group], size_ref[group + 1]

    def build(slot):
        e = slot // FAN
        w = tab_ref[e, slot % FAN]
        block = pl.ds(pl.multiple_of(e * BLOCK, BLOCK), BLOCK)
        start = pl.multiple_of(w * BLOCK, BLOCK)
        dots = lax.dot_general(
            sim_ref[block, :],
            win_ref[pl.ds(start, BLOCK), :],
            (((1,), (1,)), ((), ())),
            preferred_element_type=jnp.float32,
        )
        t = dots * (2.0 * unit) - n_ref[pl.ds((w % local) * 8, 1), :]
        t_ref[slot] = t
        m_ref[block, :] = jnp.maximum(m_ref[block, :], jnp.maximum(t[:, :LANES], t[:, LANES:]))

    def pair(i, carry):
        at = first + 2 * i
        build(order_ref[at])
        build(order_ref[jnp.minimum(at + 1, end - 1)])
        return carry

    lax.fori_loop(0, (end - first + 1) // 2, pair, 0)
    if last:
        l_ref, p_ref, u_ref, a_ref, c_ref = refs[:5]
        for e in range(2):
            block = slice(e * BLOCK, (e + 1) * BLOCK)
            high = lanes_of(jnp.max(m_ref[block, :], axis=1, keepdims=True), BLOCK)
            m_ref[block, :] = high

            def plan(k, acc):
                t = t_ref[e * 16 + k]
                high = m_ref[block, :]
                left = jnp.exp2(t[:, :LANES] - high)
                right = jnp.exp2(t[:, LANES:] - high)
                p_ref[e * 16 + k, :, :LANES] = left
                p_ref[e * 16 + k, :, LANES:] = right
                return acc + left + right

            acc = lax.fori_loop(0, size_ref[8 + e], plan, jnp.zeros((BLOCK, LANES), jnp.float32))
            acc = lanes_of(jnp.sum(acc, axis=1, keepdims=True), BLOCK)
            a_ref[block, :] = 1.0 / acc
            u_ref[block, :] = -(high + jnp.log2(acc)) - log_rows
        columns_out(tab_ref, size_ref, t_ref, p_ref, a_ref, u_ref, used_ref, c_ref, l_ref, log_rows, True)


def joined(stats_refs, log_rows):
    a, b, c, d = [ref[...] for ref in stats_refs]
    high = jnp.maximum(jnp.maximum(a, b), jnp.maximum(c, d))
    total = jnp.exp2(a - high) + jnp.exp2(b - high) + jnp.exp2(c - high) + jnp.exp2(d - high)
    return jnp.where(high > HALF_NEG, -(high + jnp.log2(total)) - log_rows, 0.0)


def sweep_kernel(
    log_rows, tab_ref, size_ref, s0, s1, s2, s3, used_ref, m_ref, t_ref, p_ref,
    l_ref, u_ref, row_ref, v_ref, b_ref, a_ref, c_ref
):
    used = used_ref[...] > 0.0
    v = jnp.where(used, joined((s0, s1, s2, s3), log_rows), 0.0)
    v_ref[...] = v
    b = jnp.exp2(v)
    b_ref[...] = b
    scaled_rows(tab_ref, size_ref, p_ref, b_ref, a_ref)
    totals = a_ref[...]
    good = jnp.logical_and(within(b), within(totals))
    u_ref[...] = -(m_ref[...] + jnp.log2(totals)) - log_rows
    a_ref[...] = 1.0 / totals

    @pl.when(jnp.logical_not(good))
    def _():
        row_pass(tab_ref, size_ref, t_ref, v_ref, m_ref, u_ref, log_rows)

    for e in range(2):
        row_ref[e : e + 1, :] = jnp.transpose(u_ref[e * BLOCK : (e + 1) * BLOCK, :])[0:1, :]
    columns_out(tab_ref, size_ref, t_ref, p_ref, a_ref, u_ref, used_ref, c_ref, l_ref, log_rows, good)


def pull_kernel(
    log_rows, back, tab_ref, size_ref, s0, s1, s2, s3, used_ref, m_ref, t_ref, p_ref, u_ref, sim_ref, win_ref,
    out_ref, real_ref, v_ref, b_ref, a_ref, tot_ref
):
    potential = joined((s0, s1, s2, s3), log_rows)
    v_ref[...] = potential
    own = real_ref.shape[0] // 2
    for i in range(own):
        for half in range(2):
            real_ref[2 * i + half : 2 * i + half + 1, :] = (
                potential[own + i : own + i + 1, half * LANES : (half + 1) * LANES] * back
            )
    v = jnp.where(used_ref[...] > 0.0, potential, 0.0)
    b = jnp.exp2(v)
    b_ref[...] = b
    a = jnp.exp2(u_ref[...] + m_ref[...] + log_rows)
    a_ref[...] = a
    good = jnp.logical_and(within(b), within(a))

    def gather(weights):
        for e in range(2):
            rows = slice(e * BLOCK, (e + 1) * BLOCK)
            out_ref[rows, :] = jnp.zeros((BLOCK, out_ref.shape[1]), jnp.float32)
            tot_ref[...] = jnp.zeros(tot_ref.shape, jnp.float32)

            def pair(i, carry):
                sides, reals = [], []
                sums = tot_ref[...]
                for k in (2 * i, 2 * i + 1):
                    w = tab_ref[e, k]
                    for value in weights(e, k, w, rows):
                        value = jnp.where(k < size_ref[8 + e], value, 0.0).astype(jnp.bfloat16)
                        sums += value.astype(jnp.float32)
                        sides.append(value)
                    reals.append(win_ref[pl.ds(pl.multiple_of(w * BLOCK, BLOCK), BLOCK), :])
                tot_ref[...] = sums
                out_ref[rows, :] += jnp.dot(
                    jnp.concatenate(sides, axis=1),
                    jnp.concatenate(reals, axis=0),
                    preferred_element_type=jnp.float32,
                )
                return carry

            lax.fori_loop(0, (size_ref[8 + e] + 1) // 2, pair, 0)
            totals = jnp.sum(tot_ref[...], axis=1, keepdims=True)
            out_ref[rows, :] = totals * sim_ref[rows, :].astype(jnp.float32) - out_ref[rows, :]

    def scaled(e, k, w, rows):
        p = p_ref[e * 16 + k]
        b = b_ref[pl.ds(w, 1), :]
        a = a_ref[rows, :]
        return p[:, :LANES] * a * b[:, :LANES], p[:, LANES:] * a * b[:, LANES:]

    def logarithmic(e, k, w, rows):
        t = t_ref[e * 16 + k]
        v = v_ref[pl.ds(w, 1), :] + log_rows
        u = u_ref[rows, :]
        return jnp.exp2(t[:, :LANES] + u + v[:, :LANES]), jnp.exp2(t[:, LANES:] + u + v[:, LANES:])

    @pl.when(good)
    def _():
        gather(scaled)

    @pl.when(jnp.logical_not(good))
    def _():
        gather(logarithmic)


def vmem():
    return pl.BlockSpec(memory_space=pltpu.VMEM)


def smem():
    return pl.BlockSpec(memory_space=pltpu.SMEM)


def shards(sim, real, pair_real, pair_count):
    replicas = lax.axis_size("rep")
    owners = lax.axis_size("blk")
    features = sim.shape[1]
    local = real.shape[0] // BLOCK
    rows_total = owners * real.shape[0]
    log_rows = math.log2(rows_total)
    unit = LOG2E / EPS / features
    mine = lax.axis_index("blk")
    rep = lax.axis_index("rep")
    fan = pair_real.shape[1]
    group = pair_real // local - mine
    group = jnp.clip(jnp.where(mine % 2 == 0, group + 1, 1 - group), 0, 2)
    table = group * local + pair_real % local
    tiles = 2 * fan
    window = 3 * local
    active = jnp.arange(fan)[None, :] < pair_count[:, None]
    ids = jnp.arange(tiles, dtype=jnp.int32)
    place = jnp.where(active, table // local, 3).reshape(-1)
    rank = jnp.sum((place * tiles + ids)[None, :] < (place * tiles + ids)[:, None], 1)
    order = jnp.sum(jnp.where(rank[:, None] == ids[None, :], ids[:, None], 0), 0)
    bounds = jnp.sum(place[:, None] < jnp.arange(4)[None, :], 0).astype(jnp.int32)
    quarters = (rep + jnp.array([0, replicas - 1, 1, 2], jnp.int32)) % replicas
    sizes = jnp.concatenate([bounds, quarters, pair_count])
    hits = (table[:, :, None] == jnp.arange(window)) & active[:, :, None]
    used = jnp.broadcast_to(jnp.any(hits, (0, 1))[:, None], (window, BLOCK)).astype(jnp.float32)

    own = real
    from_low = rep_shift(own, 1)
    from_high = rep_shift(own, -1)
    chip_own = chip_swap(own)
    core_own = core_swap(own)
    from_low, from_high, chip_own, table, order, sizes, used = lax.optimization_barrier(
        (from_low, from_high, chip_own, table, order, sizes, used)
    )
    far = rep_shift(from_low, 1)
    near = jnp.stack([from_low, from_high])
    groups = {
        1: (own, near, far),
        2: (core_own, core_swap(near), core_swap(far)),
        0: (chip_own, chip_swap(near), chip_swap(far)),
    }
    sim_norm = jnp.sum(jnp.square(sim.astype(jnp.float32)), -1) * unit

    stats_shape = jax.ShapeDtypeStruct((window, BLOCK), jnp.float32)
    potentials = (2 * BLOCK, LANES)
    column = jax.ShapeDtypeStruct(potentials, jnp.float32)
    sim_rows = pltpu.with_memory_space_constraint(sim, pltpu.HBM)
    groups[1] = (pltpu.with_memory_space_constraint(own, pltpu.HBM), near, far)
    held = []
    for group in (1, 2, 0):
        last = group == 0
        found = pl.pallas_call(
            functools.partial(group_kernel, group, log_rows, unit),
            out_shape=[
                pltpu.VMEM((tiles, BLOCK, BLOCK), jnp.float32),
                pltpu.VMEM((window * BLOCK, features), jnp.bfloat16),
                column,
            ]
            + [stats_shape, pltpu.VMEM((tiles, BLOCK, BLOCK), jnp.float32)] * last,
            in_specs=[smem()] * 3
            + [pl.BlockSpec(memory_space=pltpu.HBM)]
            + [pl.BlockSpec(memory_space=pltpu.HBM if group == 1 else pl.ANY)]
            + [pl.BlockSpec(memory_space=pl.ANY)] * 2
            + [vmem()] * (last + len(held)),
            out_specs=[vmem()] * (3 + 2 * last),
            input_output_aliases={7 + last + i: i for i in range(len(held))},
            scratch_shapes=[
                pltpu.VMEM(potentials, jnp.float32),
                pltpu.VMEM(potentials, jnp.float32),
                pltpu.VMEM((window * 8, BLOCK), jnp.float32),
            ]
            * last
            + [
                pltpu.VMEM((local * 8, BLOCK), jnp.float32),
                pltpu.VMEM(sim.shape, sim.dtype),
                pltpu.SemaphoreType.DMA((5,)),
            ],
            compiler_params=pltpu.CompilerParams(vmem_limit_bytes=8 * MIB),
            cost_estimate=pl.CostEstimate(flops=10**9, bytes_accessed=8 * MIB, transcendentals=0),
        )(table, order, sizes, sim_rows, *groups[group], *[used] * last, *held)
        held = [pltpu.with_memory_space_constraint(value, pltpu.VMEM) for value in found[:2]] + [found[2]]
    scores, window_rows, peaks = held
    stats_out = found[3]
    plan = pltpu.with_memory_space_constraint(found[4], pltpu.VMEM)

    for sweep in range(ITERS):
        if sweep:
            stats_out, sim_pot, sim_row = pl.pallas_call(
                functools.partial(sweep_kernel, log_rows),
                out_shape=[stats_shape, column, jax.ShapeDtypeStruct((2, BLOCK), jnp.float32)],
                in_specs=[smem()] * 2 + [vmem()] * 8,
                out_specs=[vmem()] * 3,
                scratch_shapes=[
                    pltpu.VMEM((window, BLOCK), jnp.float32),
                    pltpu.VMEM((window, BLOCK), jnp.float32),
                    pltpu.VMEM(potentials, jnp.float32),
                    pltpu.VMEM((window * 8, BLOCK), jnp.float32),
                ],
                compiler_params=pltpu.CompilerParams(vmem_limit_bytes=8 * MIB),
            )(table, sizes, *around, used, peaks, scores, plan)
        core = core_swap(stats_out[local:])
        chip = chip_swap(stats_out[: 2 * local])
        past_core = chip_then_core(stats_out[:local])
        past_chip = core_then_chip(stats_out[2 * local :])
        merged = jnp.concatenate(
            [
                log_add(stats_out[:local], log_add(chip[local:], past_chip)),
                log_add(stats_out[local : 2 * local], log_add(chip[:local], core[local:])),
                log_add(stats_out[2 * local :], log_add(core[:local], past_core)),
            ]
        )
        around = (merged, rep_shift(merged, 1), rep_shift(merged, -1), rep_shift(merged, 2))

    back = EPS / LOG2E
    pull, real_out = pl.pallas_call(
        functools.partial(pull_kernel, log_rows, back),
        out_shape=[
            jax.ShapeDtypeStruct(sim.shape, jnp.float32),
            jax.ShapeDtypeStruct((2 * local, LANES), jnp.float32),
        ],
        in_specs=[smem()] * 2 + [vmem()] * 11,
        out_specs=[vmem()] * 2,
        scratch_shapes=[
            pltpu.VMEM((window, BLOCK), jnp.float32),
            pltpu.VMEM((window, BLOCK), jnp.float32),
            pltpu.VMEM(potentials, jnp.float32),
            pltpu.VMEM((BLOCK, LANES), jnp.float32),
        ],
        compiler_params=pltpu.CompilerParams(vmem_limit_bytes=8 * MIB),
    )(table, sizes, *around, used, peaks, scores, plan, sim_pot, sim, window_rows)
    sim_out = (sim_row.reshape(-1) + sim_norm) * back
    return (pull, sim_out, real_out.reshape(-1))


def solution(mesh):
    in_specs = (
        P(("blk", "rep"), None),
        P("blk", "rep"),
        P(("blk", "rep"), None),
        P(("blk", "rep")),
    )
    out_specs = (P(("blk", "rep"), None), P(("blk", "rep")), P("blk"))
    return jax.shard_map(shards, mesh=mesh, in_specs=in_specs, out_specs=out_specs, check_vma=False)
```

```python
import functools
import math

import jax
import jax.numpy as jnp
from jax import lax
from jax.experimental import pallas as pl
from jax.experimental.pallas import tpu as pltpu
from jax.sharding import PartitionSpec as P

BLOCK = 256
ITERS = 3
EPS = 0.05
NEG = -1e30
LOG2E = math.log2(math.e)
LANES = 128
FAN = 16
LEAST, MOST = 2.0**-40, 2.0**40
HALF_NEG = -5e29
MIB = 1024 * 1024


def log_add(a, b):
    high = jnp.maximum(a, b)
    return high + jnp.log2(jnp.exp2(a - high) + jnp.exp2(b - high))


def across(index, owners):
    other = ((index + 1) ^ 1) - 1
    return other if 0 <= other < owners else index


def core_swap(value):
    owners = lax.axis_size("blk")
    return lax.ppermute(value, "blk", [(i, i ^ 1) for i in range(owners)])


def chip_swap(value):
    owners = lax.axis_size("blk")
    return lax.ppermute(value, "blk", [(i, across(i, owners)) for i in range(owners)])


def chip_then_core(value):
    owners = lax.axis_size("blk")
    return lax.ppermute(value, "blk", [(i, across(i, owners) ^ 1) for i in range(owners)])


def core_then_chip(value):
    owners = lax.axis_size("blk")
    return lax.ppermute(value, "blk", [(i, across(i ^ 1, owners)) for i in range(owners)])


def rep_shift(value, by):
    count = lax.axis_size("rep")
    return lax.ppermute(value, "rep", [(i, (i + by) % count) for i in range(count)])


def rep_spin(value, by):
    owners, count = lax.axis_size("blk"), lax.axis_size("rep")
    pairs = []
    for owner in range(owners):
        way = by if owner % 2 == 0 else -by
        pairs += [(owner * count + i, owner * count + (i + way) % count) for i in range(count)]
    return lax.ppermute(value, ("blk", "rep"), pairs)


def row_pass(tab_ref, size_ref, t_ref, v_ref, u_ref, log_rows):
    part = 128
    for e in range(2):
        count = size_ref[8 + e]
        for c in range(BLOCK // part):
            rows = slice(c * part, (c + 1) * part)

            def scores(k):
                return t_ref[e * 16 + k, rows, :] + v_ref[pl.ds(tab_ref[e, k], 1), :]

            def peak(k, high):
                t = scores(k)
                return jnp.maximum(high, jnp.maximum(t[:, :LANES], t[:, LANES:]))

            high = lax.fori_loop(0, count, peak, jnp.full((part, LANES), NEG, jnp.float32))
            high = jnp.broadcast_to(jnp.max(high, axis=1, keepdims=True), (part, LANES))

            def total(k, acc):
                t = scores(k)
                return acc + jnp.exp2(t[:, :LANES] - high) + jnp.exp2(t[:, LANES:] - high)

            acc = lax.fori_loop(0, count, total, jnp.zeros((part, LANES), jnp.float32))
            acc = jnp.broadcast_to(jnp.sum(acc, axis=1, keepdims=True), (part, LANES))
            u_ref[e * BLOCK + c * part : e * BLOCK + (c + 1) * part, :] = (
                -(high + jnp.log2(acc)) - log_rows
            )


def column_pass(tab_ref, size_ref, t_ref, u_ref, l_ref):
    window = l_ref.shape[0]
    row_ids = lax.broadcasted_iota(jnp.int32, (window, LANES), 0)
    stats = []
    for e in range(2):

        def tile(k, carry):
            here = row_ids == tab_ref[e, k]
            after = []
            for half in range(2):
                lanes = slice(half * LANES, (half + 1) * LANES)
                highs, sums = carry[half]
                t = t_ref[e * 16 + k, :, lanes] + u_ref[e * BLOCK : (e + 1) * BLOCK, :]
                high = jnp.max(t, axis=0, keepdims=True)
                total = jnp.sum(jnp.exp2(t - high), axis=0, keepdims=True)
                after.append((jnp.where(here, high, highs), jnp.where(here, total, sums)))
            return tuple(after)

        start = (jnp.full((window, LANES), NEG, jnp.float32), jnp.ones((window, LANES), jnp.float32))
        found = lax.fori_loop(0, size_ref[8 + e], tile, (start, start))
        stats.append([high + jnp.log2(total) for high, total in found])
    for half in range(2):
        l_ref[:, half * LANES : (half + 1) * LANES] = log_add(stats[0][half], stats[1][half])


def lanes_of(column, rows):
    return jnp.broadcast_to(column, (rows, LANES))


def scaled_columns(tab_ref, size_ref, p_ref, a_ref, c_ref):
    c_ref[...] = jnp.zeros(c_ref.shape, jnp.float32)
    for e in range(2):

        def tile(k, carry):
            a = a_ref[e * BLOCK : (e + 1) * BLOCK, :]
            p = p_ref[e * 16 + k]
            at = pl.ds(pl.multiple_of(tab_ref[e, k] * 8, 8), 8)
            for half in range(2):
                lanes = slice(half * LANES, (half + 1) * LANES)
                terms = (p[:, lanes] * a).reshape(BLOCK // 8, 8, LANES)
                c_ref[at, lanes] += jnp.sum(terms, axis=0)
            return carry

        lax.fori_loop(0, size_ref[8 + e], tile, 0)
    window = c_ref.shape[0] // 8
    return jnp.sum(c_ref[...].reshape(window, 8, BLOCK), axis=1)


def scaled_rows(tab_ref, size_ref, p_ref, b_ref, r_ref):
    for e in range(2):

        def tile(k, acc):
            p = p_ref[e * 16 + k]
            b = b_ref[pl.ds(tab_ref[e, k], 1), :]
            return acc + p[:, :LANES] * b[:, :LANES] + p[:, LANES:] * b[:, LANES:]

        acc = lax.fori_loop(0, size_ref[8 + e], tile, jnp.zeros((BLOCK, LANES), jnp.float32))
        r_ref[e * BLOCK : (e + 1) * BLOCK, :] = lanes_of(jnp.sum(acc, axis=1, keepdims=True), BLOCK)


def within(value):
    return jnp.logical_and(jnp.min(value) >= LEAST, jnp.max(value) <= MOST)


def score_tile(sim_ref, win_ref, n_ref, block, w, unit):
    dots = lax.dot_general(
        sim_ref[block, :],
        win_ref[pl.ds(pl.multiple_of(w * BLOCK, BLOCK), BLOCK), :],
        (((1,), (1,)), ((), ())),
        preferred_element_type=jnp.float32,
    )
    return dots * (2.0 * unit) - n_ref[pl.ds(w * 8, 1), :]


def score_tiles(tab_ref, size_ref, sim_ref, win_ref, n_ref, t_ref, unit):
    for e in range(2):

        def tile(k, carry):
            block = slice(e * BLOCK, (e + 1) * BLOCK)
            t_ref[e * FAN + k] = score_tile(sim_ref, win_ref, n_ref, block, tab_ref[e, k], unit)
            return carry

        lax.fori_loop(0, size_ref[8 + e], tile, 0)


def group_kernel(group, log_rows, unit, tab_ref, order_ref, size_ref, sim_hbm, own_ref, near_ref, far_ref, *refs):
    last = group == 0
    if last:
        used_ref, refs = refs[0], refs[1:]
    if group != 1:
        refs = refs[5:]
    p_ref, win_ref, m_ref, n_ref, r_ref = refs[:5]
    refs = refs[5:]
    sim_ref, sems = refs[-2:]
    rows = own_ref.shape[0]
    local = rows // BLOCK
    sources = [own_ref, near_ref.at[0], near_ref.at[1], far_ref]
    copies = [pltpu.make_async_copy(sim_hbm, sim_ref, sems.at[4])]
    for i, source in enumerate(sources):
        at = i if group == 1 else (0, 2, 1, 3)[i]
        q = pl.multiple_of(size_ref[4 + at] * LANES, LANES)
        target = win_ref.at[pl.ds(group * rows, rows), pl.ds(q, LANES)]
        copies.append(pltpu.make_async_copy(source, target, sems.at[i]))
    for copy in copies:
        copy.start()
    for copy in copies:
        copy.wait()

    ones = jnp.ones((8, LANES), jnp.bfloat16)

    def norms(i, carry):
        start = pl.multiple_of((group * local + i) * BLOCK, BLOCK)
        y = win_ref[pl.ds(start, BLOCK), :].astype(jnp.float32)
        y = y * y
        part = (y[:, :LANES] + y[:, LANES : 2 * LANES]) + (y[:, 2 * LANES : 3 * LANES] + y[:, 3 * LANES :])
        total = jnp.zeros((8, BLOCK), jnp.float32)
        for _ in range(3):
            piece = part.astype(jnp.bfloat16)
            part = part - piece.astype(jnp.float32)
            total = total + lax.dot_general(
                ones, piece, (((1,), (1,)), ((), ())), preferred_element_type=jnp.float32
            )
        n_ref[pl.ds(pl.multiple_of((group * local + i) * 8, 8), 8), :] = total * unit
        return carry

    lax.fori_loop(0, local, norms, 0, unroll=4)
    if group == 1:
        r_ref[...] = jnp.zeros(r_ref.shape, jnp.float32)
        for e in range(2):
            block = slice(e * BLOCK, (e + 1) * BLOCK)
            t = score_tile(sim_ref, win_ref, n_ref, block, tab_ref[e, 0], unit)
            high = jnp.maximum(t[:, :LANES], t[:, LANES:])
            m_ref[block, :] = lanes_of(jnp.max(high, axis=1, keepdims=True), BLOCK)
    first, end = size_ref[group], size_ref[group + 1]

    def build(at, valid):
        slot = order_ref[at]
        e = slot // FAN
        block = pl.ds(pl.multiple_of(e * BLOCK, BLOCK), BLOCK)
        t = score_tile(sim_ref, win_ref, n_ref, block, tab_ref[e, slot % FAN], unit)
        offset = m_ref[block, :]
        left = jnp.exp2(t[:, :LANES] - offset)
        right = jnp.exp2(t[:, LANES:] - offset)
        p_ref[slot, :, :LANES] = left
        p_ref[slot, :, LANES:] = right
        both = left + right
        r_ref[block, :] += both if valid is None else jnp.where(valid, both, 0.0)

    def pair(i, carry):
        at = first + 2 * i
        build(at, None)
        build(jnp.minimum(at + 1, end - 1), at + 1 < end)
        return carry

    lax.fori_loop(0, (end - first + 1) // 2, pair, 0)

    if last:
        l_ref, a_ref, c_ref, t_ref, u_ref, v_ref = refs[:6]
        good = True
        for e in range(2):
            block = slice(e * BLOCK, (e + 1) * BLOCK)
            total = lanes_of(jnp.sum(r_ref[block, :], axis=1, keepdims=True), BLOCK)
            a_ref[block, :] = 1.0 / total
            good = jnp.logical_and(good, within(total))
        good = columns_out(tab_ref, size_ref, p_ref, a_ref, used_ref, c_ref, l_ref, log_rows, good)

        @pl.when(jnp.logical_not(good))
        def _():
            v_ref[...] = jnp.zeros(v_ref.shape, jnp.float32)
            score_tiles(tab_ref, size_ref, sim_ref, win_ref, n_ref, t_ref, unit)
            row_pass(tab_ref, size_ref, t_ref, v_ref, u_ref, log_rows)
            column_pass(tab_ref, size_ref, t_ref, u_ref, l_ref)


def columns_out(tab_ref, size_ref, p_ref, a_ref, used_ref, c_ref, l_ref, log_rows, good):
    used = used_ref[...] > 0.0
    total = jnp.where(used, scaled_columns(tab_ref, size_ref, p_ref, a_ref, c_ref), 1.0)
    l_ref[...] = jnp.where(used, jnp.log2(total) - log_rows, NEG)
    return jnp.logical_and(good, within(total))


def joined(stats_refs, log_rows):
    a, b, c, d = [ref[...] for ref in stats_refs]
    high = jnp.maximum(jnp.maximum(a, b), jnp.maximum(c, d))
    total = jnp.exp2(a - high) + jnp.exp2(b - high) + jnp.exp2(c - high) + jnp.exp2(d - high)
    return jnp.where(high > HALF_NEG, -(high + jnp.log2(total)) - log_rows, 0.0)


def sweep_kernel(
    last, log_rows, unit, tab_ref, size_ref, s0, s1, s2, s3, used_ref, m_ref, n_ref, p_ref, win_ref, sim_hbm, *refs
):
    l_ref, refs = refs[0], refs[1:]
    if last:
        u_ref, row_ref, *refs = refs
        v_ref, b_ref, a_ref, c_ref, t_ref, sim_ref, sem = refs
    else:
        u_ref, v_ref, b_ref, a_ref, c_ref, t_ref, sim_ref, sem = refs
    v = jnp.where(used_ref[...] > 0.0, joined((s0, s1, s2, s3), log_rows), 0.0)
    v_ref[...] = v
    b = jnp.exp2(v)
    b_ref[...] = b
    scaled_rows(tab_ref, size_ref, p_ref, b_ref, a_ref)
    totals = a_ref[...]
    good = jnp.logical_and(within(b), within(totals))
    if last:
        u_ref[...] = -(m_ref[...] + jnp.log2(totals)) - log_rows
    a_ref[...] = 1.0 / totals
    good = columns_out(tab_ref, size_ref, p_ref, a_ref, used_ref, c_ref, l_ref, log_rows, good)

    @pl.when(jnp.logical_not(good))
    def _():
        copy = pltpu.make_async_copy(sim_hbm, sim_ref, sem)
        copy.start()
        copy.wait()
        score_tiles(tab_ref, size_ref, sim_ref, win_ref, n_ref, t_ref, unit)
        row_pass(tab_ref, size_ref, t_ref, v_ref, u_ref, log_rows)
        column_pass(tab_ref, size_ref, t_ref, u_ref, l_ref)

    if last:
        for e in range(2):
            row_ref[e : e + 1, :] = jnp.transpose(u_ref[e * BLOCK : (e + 1) * BLOCK, :])[0:1, :]


def pull_kernel(
    log_rows, back, unit, tab_ref, size_ref, s0, s1, s2, s3, used_ref, m_ref, n_ref, p_ref, u_ref, sim_ref, win_ref,
    out_ref, real_ref, v_ref, b_ref, a_ref, tot_ref, t_ref
):
    potential = joined((s0, s1, s2, s3), log_rows)
    v_ref[...] = potential
    own = real_ref.shape[0] // 2
    for i in range(own):
        for half in range(2):
            real_ref[2 * i + half : 2 * i + half + 1, :] = (
                potential[own + i : own + i + 1, half * LANES : (half + 1) * LANES] * back
            )
    v = jnp.where(used_ref[...] > 0.0, potential, 0.0)
    b = jnp.exp2(v)
    b_ref[...] = b
    a = jnp.exp2(u_ref[...] + m_ref[...] + log_rows)
    a_ref[...] = a
    good = jnp.logical_and(within(b), within(a))

    def gather(weights):
        for e in range(2):
            rows = slice(e * BLOCK, (e + 1) * BLOCK)
            count = size_ref[8 + e]
            out_ref[rows, :] = jnp.zeros((BLOCK, out_ref.shape[1]), jnp.float32)
            tot_ref[...] = jnp.zeros(tot_ref.shape, jnp.float32)

            def pair(i, carry):
                sides, reals = [], []
                sums = tot_ref[...]
                for at in (2 * i, 2 * i + 1):
                    k = jnp.minimum(at, count - 1)
                    w = tab_ref[e, k]
                    for value in weights(e, k, w, rows, at < count):
                        value = value.astype(jnp.bfloat16)
                        sums += value.astype(jnp.float32)
                        sides.append(value)
                    reals.append(win_ref[pl.ds(pl.multiple_of(w * BLOCK, BLOCK), BLOCK), :])
                tot_ref[...] = sums
                out_ref[rows, :] += jnp.dot(
                    jnp.concatenate(sides, axis=1),
                    jnp.concatenate(reals, axis=0),
                    preferred_element_type=jnp.float32,
                )
                return carry

            lax.fori_loop(0, (count + 1) // 2, pair, 0)
            totals = jnp.sum(tot_ref[...], axis=1, keepdims=True)
            out_ref[rows, :] = totals * sim_ref[rows, :].astype(jnp.float32) - out_ref[rows, :]

    def scaled(e, k, w, rows, valid):
        p = p_ref[e * FAN + k]
        b = jnp.where(valid, b_ref[pl.ds(w, 1), :], 0.0)
        a = a_ref[rows, :]
        return p[:, :LANES] * a * b[:, :LANES], p[:, LANES:] * a * b[:, LANES:]

    def logarithmic(e, k, w, rows, valid):
        t = t_ref[e * FAN + k]
        v = v_ref[pl.ds(w, 1), :] + log_rows
        u = u_ref[rows, :]
        left, right = jnp.exp2(t[:, :LANES] + u + v[:, :LANES]), jnp.exp2(t[:, LANES:] + u + v[:, LANES:])
        return jnp.where(valid, left, 0.0), jnp.where(valid, right, 0.0)

    @pl.when(good)
    def _():
        gather(scaled)

    @pl.when(jnp.logical_not(good))
    def _():
        score_tiles(tab_ref, size_ref, sim_ref, win_ref, n_ref, t_ref, unit)
        gather(logarithmic)


def vmem():
    return pl.BlockSpec(memory_space=pltpu.VMEM)


def smem():
    return pl.BlockSpec(memory_space=pltpu.SMEM)


def shards(sim, real, pair_real, pair_count):
    replicas = lax.axis_size("rep")
    owners = lax.axis_size("blk")
    features = sim.shape[1]
    local = real.shape[0] // BLOCK
    rows_total = owners * real.shape[0]
    log_rows = math.log2(rows_total)
    unit = LOG2E / EPS / features
    mine = lax.axis_index("blk")
    rep = lax.axis_index("rep")
    fan = pair_real.shape[1]
    group = pair_real // local - mine
    group = jnp.clip(jnp.where(mine % 2 == 0, group + 1, 1 - group), 0, 2)
    table = group * local + pair_real % local
    tiles = 2 * fan
    window = 3 * local
    active = jnp.arange(fan)[None, :] < pair_count[:, None]
    ids = jnp.arange(tiles, dtype=jnp.int32)
    place = jnp.where(active, table // local, 3).reshape(-1)
    rank = jnp.sum((place * tiles + ids)[None, :] < (place * tiles + ids)[:, None], 1)
    order = jnp.sum(jnp.where(rank[:, None] == ids[None, :], ids[:, None], 0), 0)
    bounds = jnp.sum(place[:, None] < jnp.arange(4)[None, :], 0).astype(jnp.int32)
    way = 1 - 2 * (mine % 2)
    quarters = (rep + replicas + jnp.array([0, -1, 1, 2], jnp.int32) * way) % replicas
    sizes = jnp.concatenate([bounds, quarters, pair_count])
    hits = (table[:, :, None] == jnp.arange(window)) & active[:, :, None]
    used = jnp.broadcast_to(jnp.any(hits, (0, 1))[:, None], (window, BLOCK)).astype(jnp.float32)

    own = real
    first = rep_spin(own, 1)
    second = rep_spin(own, -1)
    chip_own = chip_swap(own)
    core_own = core_swap(own)
    first, second, chip_own, core_own, table, order, sizes, used = lax.optimization_barrier(
        (first, second, chip_own, core_own, table, order, sizes, used)
    )
    far = rep_spin(first, 1)
    near = jnp.stack([first, second])
    groups = {
        1: (own, near, far),
        2: (core_own, core_swap(near), core_swap(far)),
        0: (chip_own, chip_swap(near), chip_swap(far)),
    }
    sim_norm = jnp.sum(jnp.square(sim.astype(jnp.float32)), -1) * unit

    stats_shape = jax.ShapeDtypeStruct((window, BLOCK), jnp.float32)
    potentials = (2 * BLOCK, LANES)
    column = jax.ShapeDtypeStruct(potentials, jnp.float32)
    sim_rows = pltpu.with_memory_space_constraint(sim, pltpu.HBM)
    groups[1] = (pltpu.with_memory_space_constraint(own, pltpu.HBM), near, far)
    plans = pltpu.VMEM((tiles, BLOCK, BLOCK), jnp.float32)
    rows_of = pltpu.VMEM((window, BLOCK), jnp.float32)
    sums_of = pltpu.VMEM((window * 8, BLOCK), jnp.float32)
    held_sim = pltpu.VMEM(sim.shape, sim.dtype)
    col = pltpu.VMEM(potentials, jnp.float32)
    held = []
    for group in (1, 2, 0):
        last = group == 0
        found = pl.pallas_call(
            functools.partial(group_kernel, group, log_rows, unit),
            out_shape=[
                plans,
                pltpu.VMEM((window * BLOCK, features), jnp.bfloat16),
                column,
                jax.ShapeDtypeStruct((window * 8, BLOCK), jnp.float32),
                column,
            ]
            + [stats_shape] * last,
            in_specs=[smem()] * 3
            + [pl.BlockSpec(memory_space=pltpu.HBM)]
            + [pl.BlockSpec(memory_space=pltpu.HBM if group == 1 else pl.ANY)]
            + [pl.BlockSpec(memory_space=pl.ANY)] * 2
            + [vmem()] * (last + len(held)),
            out_specs=[vmem()] * (5 + last),
            input_output_aliases={7 + last + i: i for i in range(len(held))},
            scratch_shapes=[col, sums_of, plans, col, rows_of] * last + [held_sim, pltpu.SemaphoreType.DMA((5,))],
            compiler_params=pltpu.CompilerParams(vmem_limit_bytes=(16 if last else 6) * MIB),
            cost_estimate=pl.CostEstimate(flops=10**9, bytes_accessed=8 * MIB, transcendentals=0),
        )(table, order, sizes, sim_rows, *groups[group], *[used] * last, *held)
        held = [pltpu.with_memory_space_constraint(value, pltpu.VMEM) for value in found[:2]] + list(found[2:5])
    plan, window_rows, peaks, norms, _ = held
    stats_out = found[5]

    for sweep in range(ITERS):
        if sweep:
            last = sweep == ITERS - 1
            found = pl.pallas_call(
                functools.partial(sweep_kernel, last, log_rows, unit),
                out_shape=[stats_shape] + [column, jax.ShapeDtypeStruct((2, BLOCK), jnp.float32)] * last,
                in_specs=[smem()] * 2 + [vmem()] * 9 + [pl.BlockSpec(memory_space=pltpu.HBM)],
                out_specs=[vmem()] * (1 + 2 * last),
                scratch_shapes=[col] * (not last)
                + [rows_of, rows_of, col, sums_of, plans, held_sim, pltpu.SemaphoreType.DMA],
                compiler_params=pltpu.CompilerParams(vmem_limit_bytes=14 * MIB),
            )(table, sizes, *around, used, peaks, norms, plan, window_rows, sim_rows)
            stats_out = found[0]
        core = core_swap(stats_out[local:])
        chip = chip_swap(stats_out[: 2 * local])
        past_core = chip_then_core(stats_out[:local])
        past_chip = core_then_chip(stats_out[2 * local :])
        merged = jnp.concatenate(
            [
                log_add(stats_out[:local], log_add(chip[local:], past_chip)),
                log_add(stats_out[local : 2 * local], log_add(chip[:local], core[local:])),
                log_add(stats_out[2 * local :], log_add(core[:local], past_core)),
            ]
        )
        around = (merged, rep_shift(merged, 1), rep_shift(merged, -1), rep_shift(merged, 2))

    sim_pot, sim_row = found[1:]
    back = EPS / LOG2E
    pull, real_out = pl.pallas_call(
        functools.partial(pull_kernel, log_rows, back, unit),
        out_shape=[
            jax.ShapeDtypeStruct(sim.shape, jnp.float32),
            jax.ShapeDtypeStruct((2 * local, LANES), jnp.float32),
        ],
        in_specs=[smem()] * 2 + [vmem()] * 11,
        out_specs=[vmem()] * 2,
        scratch_shapes=[rows_of, rows_of, col, pltpu.VMEM((BLOCK, LANES), jnp.float32), plans],
        compiler_params=pltpu.CompilerParams(vmem_limit_bytes=16 * MIB),
    )(table, sizes, *around, used, peaks, norms, plan, sim_pot, sim, window_rows)
    sim_out = (sim_row.reshape(-1) + sim_norm) * back
    return (pull, sim_out, real_out.reshape(-1))


def solution(mesh):
    in_specs = (
        P(("blk", "rep"), None),
        P("blk", "rep"),
        P(("blk", "rep"), None),
        P(("blk", "rep")),
    )
    out_specs = (P(("blk", "rep"), None), P(("blk", "rep")), P("blk"))
    return jax.shard_map(shards, mesh=mesh, in_specs=in_specs, out_specs=out_specs, check_vma=False)
```

```python
import functools
import math

import jax
import jax.numpy as jnp
from jax import lax
from jax.experimental import pallas as pl
from jax.experimental.pallas import tpu as pltpu
from jax.sharding import PartitionSpec as P

BLOCK = 256
ITERS = 3
EPS = 0.05
NEG = -1e30
LOG2E = math.log2(math.e)
LANES = 128
FAN = 16
LEAST, MOST = 2.0**-40, 2.0**40
HALF_NEG = -5e29
MIB = 1024 * 1024


def log_add(a, b):
    high = jnp.maximum(a, b)
    return high + jnp.log2(jnp.exp2(a - high) + jnp.exp2(b - high))


def across(index, owners):
    other = ((index + 1) ^ 1) - 1
    return other if 0 <= other < owners else index


def core_swap(value):
    owners = lax.axis_size("blk")
    return lax.ppermute(value, "blk", [(i, i ^ 1) for i in range(owners)])


def chip_swap(value):
    owners = lax.axis_size("blk")
    return lax.ppermute(value, "blk", [(i, across(i, owners)) for i in range(owners)])


def rep_shift(value, by):
    count = lax.axis_size("rep")
    return lax.ppermute(value, "rep", [(i, (i + by) % count) for i in range(count)])


def rep_spin(value, by):
    owners, count = lax.axis_size("blk"), lax.axis_size("rep")
    pairs = []
    for owner in range(owners):
        way = by if owner % 2 == 0 else -by
        pairs += [(owner * count + i, owner * count + (i + way) % count) for i in range(count)]
    return lax.ppermute(value, ("blk", "rep"), pairs)


def row_pass(tab_ref, size_ref, t_ref, v_ref, u_ref, log_rows):
    part = 128
    for e in range(2):
        count = size_ref[8 + e]
        for c in range(BLOCK // part):
            rows = slice(c * part, (c + 1) * part)

            def scores(k):
                return t_ref[e * 16 + k, rows, :] + v_ref[pl.ds(tab_ref[e, k], 1), :]

            def peak(k, high):
                t = scores(k)
                return jnp.maximum(high, jnp.maximum(t[:, :LANES], t[:, LANES:]))

            high = lax.fori_loop(0, count, peak, jnp.full((part, LANES), NEG, jnp.float32))
            high = jnp.broadcast_to(jnp.max(high, axis=1, keepdims=True), (part, LANES))

            def total(k, acc):
                t = scores(k)
                return acc + jnp.exp2(t[:, :LANES] - high) + jnp.exp2(t[:, LANES:] - high)

            acc = lax.fori_loop(0, count, total, jnp.zeros((part, LANES), jnp.float32))
            acc = jnp.broadcast_to(jnp.sum(acc, axis=1, keepdims=True), (part, LANES))
            u_ref[e * BLOCK + c * part : e * BLOCK + (c + 1) * part, :] = (
                -(high + jnp.log2(acc)) - log_rows
            )


def column_pass(tab_ref, size_ref, t_ref, u_ref, l_ref):
    window = l_ref.shape[0]
    row_ids = lax.broadcasted_iota(jnp.int32, (window, LANES), 0)
    stats = []
    for e in range(2):

        def tile(k, carry):
            here = row_ids == tab_ref[e, k]
            after = []
            for half in range(2):
                lanes = slice(half * LANES, (half + 1) * LANES)
                highs, sums = carry[half]
                t = t_ref[e * 16 + k, :, lanes] + u_ref[e * BLOCK : (e + 1) * BLOCK, :]
                high = jnp.max(t, axis=0, keepdims=True)
                total = jnp.sum(jnp.exp2(t - high), axis=0, keepdims=True)
                after.append((jnp.where(here, high, highs), jnp.where(here, total, sums)))
            return tuple(after)

        start = (jnp.full((window, LANES), NEG, jnp.float32), jnp.ones((window, LANES), jnp.float32))
        found = lax.fori_loop(0, size_ref[8 + e], tile, (start, start))
        stats.append([high + jnp.log2(total) for high, total in found])
    for half in range(2):
        l_ref[:, half * LANES : (half + 1) * LANES] = log_add(stats[0][half], stats[1][half])


def lanes_of(column, rows):
    return jnp.broadcast_to(column, (rows, LANES))


def scaled_columns(tab_ref, size_ref, p_ref, a_ref, c_ref):
    c_ref[...] = jnp.zeros(c_ref.shape, jnp.float32)
    for e in range(2):

        def tile(k, carry):
            a = a_ref[e * BLOCK : (e + 1) * BLOCK, :]
            p = p_ref[e * 16 + k]
            at = pl.ds(pl.multiple_of(tab_ref[e, k] * 8, 8), 8)
            for half in range(2):
                lanes = slice(half * LANES, (half + 1) * LANES)
                terms = (p[:, lanes] * a).reshape(BLOCK // 8, 8, LANES)
                c_ref[at, lanes] += jnp.sum(terms, axis=0)
            return carry

        lax.fori_loop(0, size_ref[8 + e], tile, 0)
    window = c_ref.shape[0] // 8
    return jnp.sum(c_ref[...].reshape(window, 8, BLOCK), axis=1)


def scaled_rows(tab_ref, size_ref, p_ref, b_ref, r_ref):
    for e in range(2):

        def tile(k, acc):
            p = p_ref[e * 16 + k]
            b = b_ref[pl.ds(tab_ref[e, k], 1), :]
            return acc + p[:, :LANES] * b[:, :LANES] + p[:, LANES:] * b[:, LANES:]

        acc = lax.fori_loop(0, size_ref[8 + e], tile, jnp.zeros((BLOCK, LANES), jnp.float32))
        r_ref[e * BLOCK : (e + 1) * BLOCK, :] = lanes_of(jnp.sum(acc, axis=1, keepdims=True), BLOCK)


def within(value):
    return jnp.logical_and(jnp.min(value) >= LEAST, jnp.max(value) <= MOST)


def score_tile(sim_ref, win_ref, n_ref, block, w, unit):
    dots = lax.dot_general(
        sim_ref[block, :],
        win_ref[pl.ds(pl.multiple_of(w * BLOCK, BLOCK), BLOCK), :],
        (((1,), (1,)), ((), ())),
        preferred_element_type=jnp.float32,
    )
    return dots * (2.0 * unit) - n_ref[pl.ds(w * 8, 1), :]


def score_tiles(tab_ref, size_ref, sim_ref, win_ref, n_ref, t_ref, unit):
    for e in range(2):

        def tile(k, carry):
            block = slice(e * BLOCK, (e + 1) * BLOCK)
            t_ref[e * FAN + k] = score_tile(sim_ref, win_ref, n_ref, block, tab_ref[e, k], unit)
            return carry

        lax.fori_loop(0, size_ref[8 + e], tile, 0)


def group_kernel(group, log_rows, unit, tab_ref, order_ref, size_ref, sim_hbm, own_ref, near_ref, far_ref, *refs):
    last = group == 0
    if last:
        used_ref, refs = refs[0], refs[1:]
    if group != 1:
        refs = refs[5:]
    p_ref, win_ref, m_ref, n_ref, r_ref = refs[:5]
    refs = refs[5:]
    sim_ref, sems = refs[-2:]
    rows = own_ref.shape[0]
    local = rows // BLOCK
    sources = [own_ref, near_ref.at[0], near_ref.at[1], far_ref]
    copies = [pltpu.make_async_copy(sim_hbm, sim_ref, sems.at[4])]
    for i, source in enumerate(sources):
        at = i if group == 1 else (0, 2, 1, 3)[i]
        q = pl.multiple_of(size_ref[4 + at] * LANES, LANES)
        target = win_ref.at[pl.ds(group * rows, rows), pl.ds(q, LANES)]
        copies.append(pltpu.make_async_copy(source, target, sems.at[i]))
    for copy in copies:
        copy.start()
    for copy in copies:
        copy.wait()

    ones = jnp.ones((8, LANES), jnp.bfloat16)

    def norms(i, carry):
        start = pl.multiple_of((group * local + i) * BLOCK, BLOCK)
        y = win_ref[pl.ds(start, BLOCK), :].astype(jnp.float32)
        y = y * y
        part = (y[:, :LANES] + y[:, LANES : 2 * LANES]) + (y[:, 2 * LANES : 3 * LANES] + y[:, 3 * LANES :])
        total = jnp.zeros((8, BLOCK), jnp.float32)
        for _ in range(3):
            piece = part.astype(jnp.bfloat16)
            part = part - piece.astype(jnp.float32)
            total = total + lax.dot_general(
                ones, piece, (((1,), (1,)), ((), ())), preferred_element_type=jnp.float32
            )
        n_ref[pl.ds(pl.multiple_of((group * local + i) * 8, 8), 8), :] = total * unit
        return carry

    lax.fori_loop(0, local, norms, 0, unroll=4)
    if group == 1:
        r_ref[...] = jnp.zeros(r_ref.shape, jnp.float32)
        for e in range(2):
            block = slice(e * BLOCK, (e + 1) * BLOCK)
            t = score_tile(sim_ref, win_ref, n_ref, block, tab_ref[e, 0], unit)
            high = jnp.maximum(t[:, :LANES], t[:, LANES:])
            m_ref[block, :] = lanes_of(jnp.max(high, axis=1, keepdims=True), BLOCK)
    first, end = size_ref[group], size_ref[group + 1]

    def build(at, valid):
        slot = order_ref[at]
        e = slot // FAN
        block = pl.ds(pl.multiple_of(e * BLOCK, BLOCK), BLOCK)
        t = score_tile(sim_ref, win_ref, n_ref, block, tab_ref[e, slot % FAN], unit)
        offset = m_ref[block, :]
        left = jnp.exp2(t[:, :LANES] - offset)
        right = jnp.exp2(t[:, LANES:] - offset)
        p_ref[slot, :, :LANES] = left
        p_ref[slot, :, LANES:] = right
        both = left + right
        r_ref[block, :] += both if valid is None else jnp.where(valid, both, 0.0)

    def pair(i, carry):
        at = first + 2 * i
        build(at, None)
        build(jnp.minimum(at + 1, end - 1), at + 1 < end)
        return carry

    lax.fori_loop(0, (end - first + 1) // 2, pair, 0)

    if last:
        l_ref, a_ref, c_ref, t_ref, u_ref, v_ref = refs[:6]
        good = True
        for e in range(2):
            block = slice(e * BLOCK, (e + 1) * BLOCK)
            total = lanes_of(jnp.sum(r_ref[block, :], axis=1, keepdims=True), BLOCK)
            a_ref[block, :] = 1.0 / total
            good = jnp.logical_and(good, within(total))
        good = columns_out(tab_ref, size_ref, p_ref, a_ref, used_ref, c_ref, l_ref, log_rows, good)

        @pl.when(jnp.logical_not(good))
        def _():
            v_ref[...] = jnp.zeros(v_ref.shape, jnp.float32)
            score_tiles(tab_ref, size_ref, sim_ref, win_ref, n_ref, t_ref, unit)
            row_pass(tab_ref, size_ref, t_ref, v_ref, u_ref, log_rows)
            column_pass(tab_ref, size_ref, t_ref, u_ref, l_ref)


def columns_out(tab_ref, size_ref, p_ref, a_ref, used_ref, c_ref, l_ref, log_rows, good):
    used = used_ref[...] > 0.0
    total = jnp.where(used, scaled_columns(tab_ref, size_ref, p_ref, a_ref, c_ref), 1.0)
    l_ref[...] = jnp.where(used, jnp.log2(total) - log_rows, NEG)
    return jnp.logical_and(good, within(total))


def joined(stats_refs, log_rows):
    a, b, c, d = [ref[...] for ref in stats_refs]
    high = jnp.maximum(jnp.maximum(a, b), jnp.maximum(c, d))
    total = jnp.exp2(a - high) + jnp.exp2(b - high) + jnp.exp2(c - high) + jnp.exp2(d - high)
    return jnp.where(high > HALF_NEG, -(high + jnp.log2(total)) - log_rows, 0.0)


def sweep_kernel(
    last, log_rows, unit, tab_ref, size_ref, s0, s1, s2, s3, used_ref, m_ref, n_ref, p_ref, win_ref, sim_hbm, *refs
):
    l_ref, refs = refs[0], refs[1:]
    if last:
        u_ref, row_ref, *refs = refs
        v_ref, b_ref, a_ref, c_ref, t_ref, sim_ref, sem = refs
    else:
        u_ref, v_ref, b_ref, a_ref, c_ref, t_ref, sim_ref, sem = refs
    v = jnp.where(used_ref[...] > 0.0, joined((s0, s1, s2, s3), log_rows), 0.0)
    v_ref[...] = v
    b = jnp.exp2(v)
    b_ref[...] = b
    scaled_rows(tab_ref, size_ref, p_ref, b_ref, a_ref)
    totals = a_ref[...]
    good = jnp.logical_and(within(b), within(totals))
    if last:
        u_ref[...] = -(m_ref[...] + jnp.log2(totals)) - log_rows
    a_ref[...] = 1.0 / totals
    good = columns_out(tab_ref, size_ref, p_ref, a_ref, used_ref, c_ref, l_ref, log_rows, good)

    @pl.when(jnp.logical_not(good))
    def _():
        copy = pltpu.make_async_copy(sim_hbm, sim_ref, sem)
        copy.start()
        copy.wait()
        score_tiles(tab_ref, size_ref, sim_ref, win_ref, n_ref, t_ref, unit)
        row_pass(tab_ref, size_ref, t_ref, v_ref, u_ref, log_rows)
        column_pass(tab_ref, size_ref, t_ref, u_ref, l_ref)

    if last:
        for e in range(2):
            row_ref[e : e + 1, :] = jnp.transpose(u_ref[e * BLOCK : (e + 1) * BLOCK, :])[0:1, :]


def pull_kernel(
    log_rows, back, unit, tab_ref, size_ref, s0, s1, s2, s3, used_ref, m_ref, n_ref, p_ref, u_ref, sim_ref, win_ref,
    out_ref, real_ref, v_ref, b_ref, a_ref, tot_ref, t_ref
):
    potential = joined((s0, s1, s2, s3), log_rows)
    v_ref[...] = potential
    own = real_ref.shape[0] // 2
    for i in range(own):
        for half in range(2):
            real_ref[2 * i + half : 2 * i + half + 1, :] = (
                potential[own + i : own + i + 1, half * LANES : (half + 1) * LANES] * back
            )
    v = jnp.where(used_ref[...] > 0.0, potential, 0.0)
    b = jnp.exp2(v)
    b_ref[...] = b
    a = jnp.exp2(u_ref[...] + m_ref[...] + log_rows)
    a_ref[...] = a
    good = jnp.logical_and(within(b), within(a))

    def gather(weights):
        for e in range(2):
            rows = slice(e * BLOCK, (e + 1) * BLOCK)
            count = size_ref[8 + e]
            out_ref[rows, :] = jnp.zeros((BLOCK, out_ref.shape[1]), jnp.float32)
            tot_ref[...] = jnp.zeros(tot_ref.shape, jnp.float32)

            def pair(i, carry):
                sides, reals = [], []
                sums = tot_ref[...]
                for at in (2 * i, 2 * i + 1):
                    k = jnp.minimum(at, count - 1)
                    w = tab_ref[e, k]
                    for value in weights(e, k, w, rows, at < count):
                        value = value.astype(jnp.bfloat16)
                        sums += value.astype(jnp.float32)
                        sides.append(value)
                    reals.append(win_ref[pl.ds(pl.multiple_of(w * BLOCK, BLOCK), BLOCK), :])
                tot_ref[...] = sums
                out_ref[rows, :] += jnp.dot(
                    jnp.concatenate(sides, axis=1),
                    jnp.concatenate(reals, axis=0),
                    preferred_element_type=jnp.float32,
                )
                return carry

            lax.fori_loop(0, (count + 1) // 2, pair, 0)
            totals = jnp.sum(tot_ref[...], axis=1, keepdims=True)
            out_ref[rows, :] = totals * sim_ref[rows, :].astype(jnp.float32) - out_ref[rows, :]

    def scaled(e, k, w, rows, valid):
        p = p_ref[e * FAN + k]
        b = jnp.where(valid, b_ref[pl.ds(w, 1), :], 0.0)
        a = a_ref[rows, :]
        return p[:, :LANES] * a * b[:, :LANES], p[:, LANES:] * a * b[:, LANES:]

    def logarithmic(e, k, w, rows, valid):
        t = t_ref[e * FAN + k]
        v = v_ref[pl.ds(w, 1), :] + log_rows
        u = u_ref[rows, :]
        left, right = jnp.exp2(t[:, :LANES] + u + v[:, :LANES]), jnp.exp2(t[:, LANES:] + u + v[:, LANES:])
        return jnp.where(valid, left, 0.0), jnp.where(valid, right, 0.0)

    @pl.when(good)
    def _():
        gather(scaled)

    @pl.when(jnp.logical_not(good))
    def _():
        score_tiles(tab_ref, size_ref, sim_ref, win_ref, n_ref, t_ref, unit)
        gather(logarithmic)


def vmem():
    return pl.BlockSpec(memory_space=pltpu.VMEM)


def smem():
    return pl.BlockSpec(memory_space=pltpu.SMEM)


def shards(sim, real, pair_real, pair_count):
    replicas = lax.axis_size("rep")
    owners = lax.axis_size("blk")
    features = sim.shape[1]
    local = real.shape[0] // BLOCK
    rows_total = owners * real.shape[0]
    log_rows = math.log2(rows_total)
    unit = LOG2E / EPS / features
    mine = lax.axis_index("blk")
    rep = lax.axis_index("rep")
    fan = pair_real.shape[1]
    group = pair_real // local - mine
    group = jnp.clip(jnp.where(mine % 2 == 0, group + 1, 1 - group), 0, 2)
    table = group * local + pair_real % local
    tiles = 2 * fan
    window = 3 * local
    active = jnp.arange(fan)[None, :] < pair_count[:, None]
    ids = jnp.arange(tiles, dtype=jnp.int32)
    place = jnp.where(active, table // local, 3).reshape(-1)
    rank = jnp.sum((place * tiles + ids)[None, :] < (place * tiles + ids)[:, None], 1)
    order = jnp.sum(jnp.where(rank[:, None] == ids[None, :], ids[:, None], 0), 0)
    bounds = jnp.sum(place[:, None] < jnp.arange(4)[None, :], 0).astype(jnp.int32)
    way = 1 - 2 * (mine % 2)
    quarters = (rep + replicas + jnp.array([0, -1, 1, 2], jnp.int32) * way) % replicas
    sizes = jnp.concatenate([bounds, quarters, pair_count])
    hits = (table[:, :, None] == jnp.arange(window)) & active[:, :, None]
    used = jnp.broadcast_to(jnp.any(hits, (0, 1))[:, None], (window, BLOCK)).astype(jnp.float32)

    own = real
    first = rep_spin(own, 1)
    second = rep_spin(own, -1)
    chip_own = chip_swap(own)
    core_own = core_swap(own)
    first, second, chip_own, core_own, table, order, sizes, used = lax.optimization_barrier(
        (first, second, chip_own, core_own, table, order, sizes, used)
    )
    far = rep_spin(first, 1)
    near = jnp.stack([first, second])
    groups = {
        1: (own, near, far),
        2: (core_own, core_swap(near), core_swap(far)),
        0: (chip_own, chip_swap(near), chip_swap(far)),
    }
    sim_norm = jnp.sum(jnp.square(sim.astype(jnp.float32)), -1) * unit

    stats_shape = jax.ShapeDtypeStruct((window, BLOCK), jnp.float32)
    potentials = (2 * BLOCK, LANES)
    column = jax.ShapeDtypeStruct(potentials, jnp.float32)
    sim_rows = pltpu.with_memory_space_constraint(sim, pltpu.HBM)
    groups[1] = (pltpu.with_memory_space_constraint(own, pltpu.HBM), near, far)
    plans = pltpu.VMEM((tiles, BLOCK, BLOCK), jnp.float32)
    rows_of = pltpu.VMEM((window, BLOCK), jnp.float32)
    sums_of = pltpu.VMEM((window * 8, BLOCK), jnp.float32)
    held_sim = pltpu.VMEM(sim.shape, sim.dtype)
    col = pltpu.VMEM(potentials, jnp.float32)
    held = []
    for group in (1, 2, 0):
        last = group == 0
        found = pl.pallas_call(
            functools.partial(group_kernel, group, log_rows, unit),
            out_shape=[
                plans,
                pltpu.VMEM((window * BLOCK, features), jnp.bfloat16),
                column,
                jax.ShapeDtypeStruct((window * 8, BLOCK), jnp.float32),
                column,
            ]
            + [stats_shape] * last,
            in_specs=[smem()] * 3
            + [pl.BlockSpec(memory_space=pltpu.HBM)]
            + [pl.BlockSpec(memory_space=pltpu.HBM if group == 1 else pl.ANY)]
            + [pl.BlockSpec(memory_space=pl.ANY)] * 2
            + [vmem()] * (last + len(held)),
            out_specs=[vmem()] * (5 + last),
            input_output_aliases={7 + last + i: i for i in range(len(held))},
            scratch_shapes=[col, sums_of, plans, col, rows_of] * last + [held_sim, pltpu.SemaphoreType.DMA((5,))],
            compiler_params=pltpu.CompilerParams(vmem_limit_bytes=(16 if last else 6) * MIB),
            cost_estimate=pl.CostEstimate(flops=10**9, bytes_accessed=8 * MIB, transcendentals=0),
        )(table, order, sizes, sim_rows, *groups[group], *[used] * last, *held)
        held = [pltpu.with_memory_space_constraint(value, pltpu.VMEM) for value in found[:2]] + list(found[2:5])
    plan, window_rows, peaks, norms, _ = held
    stats_out = found[5]

    for sweep in range(ITERS):
        if sweep:
            last = sweep == ITERS - 1
            found = pl.pallas_call(
                functools.partial(sweep_kernel, last, log_rows, unit),
                out_shape=[stats_shape] + [column, jax.ShapeDtypeStruct((2, BLOCK), jnp.float32)] * last,
                in_specs=[smem()] * 2 + [vmem()] * 9 + [pl.BlockSpec(memory_space=pltpu.HBM)],
                out_specs=[vmem()] * (1 + 2 * last),
                scratch_shapes=[col] * (not last)
                + [rows_of, rows_of, col, sums_of, plans, held_sim, pltpu.SemaphoreType.DMA],
                compiler_params=pltpu.CompilerParams(vmem_limit_bytes=14 * MIB),
            )(table, sizes, *around, used, peaks, norms, plan, window_rows, sim_rows)
            stats_out = found[0]
        own_sum = log_add(stats_out[local : 2 * local], core_swap(stats_out[2 * local :]))
        chip = chip_swap(jnp.concatenate([own_sum, stats_out[:local]]))
        own_sum, chip_sum = log_add(own_sum, chip[local:]), log_add(stats_out[:local], chip[:local])
        merged = jnp.concatenate([chip_sum, own_sum, core_swap(own_sum)])
        around = (merged, rep_shift(merged, 1), rep_shift(merged, -1), rep_shift(merged, 2))

    sim_pot, sim_row = found[1:]
    back = EPS / LOG2E
    pull, real_out = pl.pallas_call(
        functools.partial(pull_kernel, log_rows, back, unit),
        out_shape=[
            jax.ShapeDtypeStruct(sim.shape, jnp.float32),
            jax.ShapeDtypeStruct((2 * local, LANES), jnp.float32),
        ],
        in_specs=[smem()] * 2 + [vmem()] * 11,
        out_specs=[vmem()] * 2,
        scratch_shapes=[rows_of, rows_of, col, pltpu.VMEM((BLOCK, LANES), jnp.float32), plans],
        compiler_params=pltpu.CompilerParams(vmem_limit_bytes=16 * MIB),
    )(table, sizes, *around, used, peaks, norms, plan, sim_pot, sim, window_rows)
    sim_out = (sim_row.reshape(-1) + sim_norm) * back
    return (pull, sim_out, real_out.reshape(-1))


def solution(mesh):
    in_specs = (
        P(("blk", "rep"), None),
        P("blk", "rep"),
        P(("blk", "rep"), None),
        P(("blk", "rep")),
    )
    out_specs = (P(("blk", "rep"), None), P(("blk", "rep")), P("blk"))
    return jax.shard_map(shards, mesh=mesh, in_specs=in_specs, out_specs=out_specs, check_vma=False)
```

```python
import functools
import math

import jax
import jax.numpy as jnp
from jax import lax
from jax.experimental import pallas as pl
from jax.experimental.pallas import tpu as pltpu
from jax.sharding import PartitionSpec as P

BLOCK = 256
ITERS = 3
EPS = 0.05
NEG = -1e30
LOG2E = math.log2(math.e)
LANES = 128
FAN = 16
LEAST, MOST = 2.0**-40, 2.0**40
HALF_NEG = -5e29
MIB = 1024 * 1024


def log_add(a, b):
    high = jnp.maximum(a, b)
    return high + jnp.log2(jnp.exp2(a - high) + jnp.exp2(b - high))


def across(index, owners):
    other = ((index + 1) ^ 1) - 1
    return other if 0 <= other < owners else index


def core_swap(value):
    owners = lax.axis_size("blk")
    return lax.ppermute(value, "blk", [(i, i ^ 1) for i in range(owners)])


def chip_swap(value):
    owners = lax.axis_size("blk")
    return lax.ppermute(value, "blk", [(i, across(i, owners)) for i in range(owners)])


def rep_shift(value, by):
    count = lax.axis_size("rep")
    return lax.ppermute(value, "rep", [(i, (i + by) % count) for i in range(count)])


def rep_spin(value, by):
    owners, count = lax.axis_size("blk"), lax.axis_size("rep")
    pairs = []
    for owner in range(owners):
        way = by if owner % 2 == 0 else -by
        pairs += [(owner * count + i, owner * count + (i + way) % count) for i in range(count)]
    return lax.ppermute(value, ("blk", "rep"), pairs)


def row_pass(tab_ref, size_ref, t_ref, v_ref, u_ref, log_rows):
    part = 128
    for e in range(2):
        count = size_ref[8 + e]
        for c in range(BLOCK // part):
            rows = slice(c * part, (c + 1) * part)

            def scores(k):
                return t_ref[e * 16 + k, rows, :] + v_ref[pl.ds(tab_ref[e, k], 1), :]

            def peak(k, high):
                t = scores(k)
                return jnp.maximum(high, jnp.maximum(t[:, :LANES], t[:, LANES:]))

            high = lax.fori_loop(0, count, peak, jnp.full((part, LANES), NEG, jnp.float32))
            high = jnp.broadcast_to(jnp.max(high, axis=1, keepdims=True), (part, LANES))

            def total(k, acc):
                t = scores(k)
                return acc + jnp.exp2(t[:, :LANES] - high) + jnp.exp2(t[:, LANES:] - high)

            acc = lax.fori_loop(0, count, total, jnp.zeros((part, LANES), jnp.float32))
            acc = jnp.broadcast_to(jnp.sum(acc, axis=1, keepdims=True), (part, LANES))
            u_ref[e * BLOCK + c * part : e * BLOCK + (c + 1) * part, :] = (
                -(high + jnp.log2(acc)) - log_rows
            )


def column_pass(tab_ref, size_ref, t_ref, u_ref, l_ref):
    window = l_ref.shape[0]
    row_ids = lax.broadcasted_iota(jnp.int32, (window, LANES), 0)
    stats = []
    for e in range(2):

        def tile(k, carry):
            here = row_ids == tab_ref[e, k]
            after = []
            for half in range(2):
                lanes = slice(half * LANES, (half + 1) * LANES)
                highs, sums = carry[half]
                t = t_ref[e * 16 + k, :, lanes] + u_ref[e * BLOCK : (e + 1) * BLOCK, :]
                high = jnp.max(t, axis=0, keepdims=True)
                total = jnp.sum(jnp.exp2(t - high), axis=0, keepdims=True)
                after.append((jnp.where(here, high, highs), jnp.where(here, total, sums)))
            return tuple(after)

        start = (jnp.full((window, LANES), NEG, jnp.float32), jnp.ones((window, LANES), jnp.float32))
        found = lax.fori_loop(0, size_ref[8 + e], tile, (start, start))
        stats.append([high + jnp.log2(total) for high, total in found])
    for half in range(2):
        l_ref[:, half * LANES : (half + 1) * LANES] = log_add(stats[0][half], stats[1][half])


def lanes_of(column, rows):
    return jnp.broadcast_to(column, (rows, LANES))


def scaled_columns(tab_ref, size_ref, p_ref, a_ref, c_ref):
    c_ref[...] = jnp.zeros(c_ref.shape, jnp.float32)
    for e in range(2):
        count = size_ref[8 + e]

        def pair(i, carry):
            a = a_ref[e * BLOCK : (e + 1) * BLOCK, :]
            for at in (2 * i, 2 * i + 1):
                k = jnp.minimum(at, count - 1)
                p = p_ref[e * FAN + k]
                rows = pl.ds(pl.multiple_of(tab_ref[e, k] * 8, 8), 8)
                for half in range(2):
                    lanes = slice(half * LANES, (half + 1) * LANES)
                    terms = jnp.sum((p[:, lanes] * a).reshape(BLOCK // 8, 8, LANES), axis=0)
                    c_ref[rows, lanes] += jnp.where(at < count, terms, 0.0)
            return carry

        lax.fori_loop(0, (count + 1) // 2, pair, 0)
    window = c_ref.shape[0] // 8
    return jnp.sum(c_ref[...].reshape(window, 8, BLOCK), axis=1)


def scaled_rows(tab_ref, size_ref, p_ref, b_ref, r_ref):
    for e in range(2):
        count = size_ref[8 + e]

        def pair(i, acc):
            for at in (2 * i, 2 * i + 1):
                k = jnp.minimum(at, count - 1)
                p = p_ref[e * FAN + k]
                b = jnp.where(at < count, b_ref[pl.ds(tab_ref[e, k], 1), :], 0.0)
                acc = acc + p[:, :LANES] * b[:, :LANES] + p[:, LANES:] * b[:, LANES:]
            return acc

        acc = lax.fori_loop(0, (count + 1) // 2, pair, jnp.zeros((BLOCK, LANES), jnp.float32))
        r_ref[e * BLOCK : (e + 1) * BLOCK, :] = lanes_of(jnp.sum(acc, axis=1, keepdims=True), BLOCK)


def within(value):
    return jnp.logical_and(jnp.min(value) >= LEAST, jnp.max(value) <= MOST)


def score_tile(sim_ref, win_ref, n_ref, block, w, unit):
    dots = lax.dot_general(
        sim_ref[block, :],
        win_ref[pl.ds(pl.multiple_of(w * BLOCK, BLOCK), BLOCK), :],
        (((1,), (1,)), ((), ())),
        preferred_element_type=jnp.float32,
    )
    return dots * (2.0 * unit) - n_ref[pl.ds(w * 8, 1), :]


def score_tiles(tab_ref, size_ref, sim_ref, win_ref, n_ref, t_ref, unit):
    for e in range(2):

        def tile(k, carry):
            block = slice(e * BLOCK, (e + 1) * BLOCK)
            t_ref[e * FAN + k] = score_tile(sim_ref, win_ref, n_ref, block, tab_ref[e, k], unit)
            return carry

        lax.fori_loop(0, size_ref[8 + e], tile, 0)


def group_kernel(group, log_rows, unit, tab_ref, order_ref, size_ref, sim_hbm, own_ref, near_ref, far_ref, *refs):
    last = group == 0
    if last:
        used_ref, refs = refs[0], refs[1:]
    if group != 1:
        refs = refs[5:]
    p_ref, win_ref, m_ref, n_ref, r_ref = refs[:5]
    refs = refs[5:]
    sim_ref, sems = refs[-2:]
    rows = own_ref.shape[0]
    local = rows // BLOCK
    sources = [own_ref, near_ref.at[0], near_ref.at[1], far_ref]
    copies = [pltpu.make_async_copy(sim_hbm, sim_ref, sems.at[4])]
    for i, source in enumerate(sources):
        at = i if group == 1 else (0, 2, 1, 3)[i]
        q = pl.multiple_of(size_ref[4 + at] * LANES, LANES)
        target = win_ref.at[pl.ds(group * rows, rows), pl.ds(q, LANES)]
        copies.append(pltpu.make_async_copy(source, target, sems.at[i]))
    for copy in copies:
        copy.start()
    for copy in copies:
        copy.wait()

    ones = jnp.ones((8, LANES), jnp.bfloat16)

    def norms(i, carry):
        start = pl.multiple_of((group * local + i) * BLOCK, BLOCK)
        y = win_ref[pl.ds(start, BLOCK), :].astype(jnp.float32)
        y = y * y
        part = (y[:, :LANES] + y[:, LANES : 2 * LANES]) + (y[:, 2 * LANES : 3 * LANES] + y[:, 3 * LANES :])
        total = jnp.zeros((8, BLOCK), jnp.float32)
        for _ in range(3):
            piece = part.astype(jnp.bfloat16)
            part = part - piece.astype(jnp.float32)
            total = total + lax.dot_general(
                ones, piece, (((1,), (1,)), ((), ())), preferred_element_type=jnp.float32
            )
        n_ref[pl.ds(pl.multiple_of((group * local + i) * 8, 8), 8), :] = total * unit
        return carry

    lax.fori_loop(0, local, norms, 0, unroll=4)
    if group == 1:
        r_ref[...] = jnp.zeros(r_ref.shape, jnp.float32)
        for e in range(2):
            block = slice(e * BLOCK, (e + 1) * BLOCK)
            t = score_tile(sim_ref, win_ref, n_ref, block, tab_ref[e, 0], unit)
            high = jnp.maximum(t[:, :LANES], t[:, LANES:])
            m_ref[block, :] = lanes_of(jnp.max(high, axis=1, keepdims=True), BLOCK)
    first, end = size_ref[group], size_ref[group + 1]

    def build(at, valid):
        slot = order_ref[at]
        e = slot // FAN
        block = pl.ds(pl.multiple_of(e * BLOCK, BLOCK), BLOCK)
        t = score_tile(sim_ref, win_ref, n_ref, block, tab_ref[e, slot % FAN], unit)
        offset = m_ref[block, :]
        left = jnp.exp2(t[:, :LANES] - offset)
        right = jnp.exp2(t[:, LANES:] - offset)
        p_ref[slot, :, :LANES] = left
        p_ref[slot, :, LANES:] = right
        both = left + right
        r_ref[block, :] += both if valid is None else jnp.where(valid, both, 0.0)

    def four(i, carry):
        at = first + 4 * i
        build(at, None)
        build(jnp.minimum(at + 1, end - 1), at + 1 < end)
        build(jnp.minimum(at + 2, end - 1), at + 2 < end)
        build(jnp.minimum(at + 3, end - 1), at + 3 < end)
        return carry

    lax.fori_loop(0, (end - first + 3) // 4, four, 0)

    if last:
        l_ref, a_ref, c_ref, t_ref, u_ref, v_ref = refs[:6]
        good = True
        for e in range(2):
            block = slice(e * BLOCK, (e + 1) * BLOCK)
            total = lanes_of(jnp.sum(r_ref[block, :], axis=1, keepdims=True), BLOCK)
            a_ref[block, :] = 1.0 / total
            good = jnp.logical_and(good, within(total))
        good = columns_out(tab_ref, size_ref, p_ref, a_ref, used_ref, c_ref, l_ref, log_rows, good)

        @pl.when(jnp.logical_not(good))
        def _():
            v_ref[...] = jnp.zeros(v_ref.shape, jnp.float32)
            score_tiles(tab_ref, size_ref, sim_ref, win_ref, n_ref, t_ref, unit)
            row_pass(tab_ref, size_ref, t_ref, v_ref, u_ref, log_rows)
            column_pass(tab_ref, size_ref, t_ref, u_ref, l_ref)


def columns_out(tab_ref, size_ref, p_ref, a_ref, used_ref, c_ref, l_ref, log_rows, good):
    used = used_ref[...] > 0.0
    total = jnp.where(used, scaled_columns(tab_ref, size_ref, p_ref, a_ref, c_ref), 1.0)
    l_ref[...] = jnp.where(used, jnp.log2(total) - log_rows, NEG)
    return jnp.logical_and(good, within(total))


def joined(stats_refs, log_rows):
    a, b, c, d = [ref[...] for ref in stats_refs]
    high = jnp.maximum(jnp.maximum(a, b), jnp.maximum(c, d))
    total = jnp.exp2(a - high) + jnp.exp2(b - high) + jnp.exp2(c - high) + jnp.exp2(d - high)
    return jnp.where(high > HALF_NEG, -(high + jnp.log2(total)) - log_rows, 0.0)


def sweep_kernel(
    last, log_rows, unit, tab_ref, size_ref, s0, s1, s2, s3, used_ref, m_ref, n_ref, p_ref, win_ref, sim_hbm, *refs
):
    l_ref, refs = refs[0], refs[1:]
    if last:
        u_ref, row_ref, *refs = refs
        v_ref, b_ref, a_ref, c_ref, t_ref, sim_ref, sem = refs
    else:
        u_ref, v_ref, b_ref, a_ref, c_ref, t_ref, sim_ref, sem = refs
    v = jnp.where(used_ref[...] > 0.0, joined((s0, s1, s2, s3), log_rows), 0.0)
    v_ref[...] = v
    b = jnp.exp2(v)
    b_ref[...] = b
    scaled_rows(tab_ref, size_ref, p_ref, b_ref, a_ref)
    totals = a_ref[...]
    good = jnp.logical_and(within(b), within(totals))
    if last:
        u_ref[...] = -(m_ref[...] + jnp.log2(totals)) - log_rows
    a_ref[...] = 1.0 / totals
    good = columns_out(tab_ref, size_ref, p_ref, a_ref, used_ref, c_ref, l_ref, log_rows, good)

    @pl.when(jnp.logical_not(good))
    def _():
        copy = pltpu.make_async_copy(sim_hbm, sim_ref, sem)
        copy.start()
        copy.wait()
        score_tiles(tab_ref, size_ref, sim_ref, win_ref, n_ref, t_ref, unit)
        row_pass(tab_ref, size_ref, t_ref, v_ref, u_ref, log_rows)
        column_pass(tab_ref, size_ref, t_ref, u_ref, l_ref)

    if last:
        for e in range(2):
            row_ref[e : e + 1, :] = jnp.transpose(u_ref[e * BLOCK : (e + 1) * BLOCK, :])[0:1, :]


def pull_kernel(
    log_rows, back, unit, tab_ref, size_ref, s0, s1, s2, s3, used_ref, m_ref, n_ref, p_ref, u_ref, sim_ref, win_ref,
    out_ref, real_ref, v_ref, b_ref, a_ref, tot_ref, t_ref
):
    potential = joined((s0, s1, s2, s3), log_rows)
    v_ref[...] = potential
    own = real_ref.shape[0] // 2
    for i in range(own):
        for half in range(2):
            real_ref[2 * i + half : 2 * i + half + 1, :] = (
                potential[own + i : own + i + 1, half * LANES : (half + 1) * LANES] * back
            )
    v = jnp.where(used_ref[...] > 0.0, potential, 0.0)
    b = jnp.exp2(v)
    b_ref[...] = b
    a = jnp.exp2(u_ref[...] + m_ref[...] + log_rows)
    a_ref[...] = a
    good = jnp.logical_and(within(b), within(a))

    def gather(weights):
        for e in range(2):
            rows = slice(e * BLOCK, (e + 1) * BLOCK)
            count = size_ref[8 + e]
            out_ref[rows, :] = jnp.zeros((BLOCK, out_ref.shape[1]), jnp.float32)
            tot_ref[...] = jnp.zeros(tot_ref.shape, jnp.float32)

            def four(i, carry):
                sides, reals = [], []
                sums = tot_ref[...]
                for at in (4 * i, 4 * i + 1, 4 * i + 2, 4 * i + 3):
                    k = jnp.minimum(at, count - 1)
                    w = tab_ref[e, k]
                    for value in weights(e, k, w, rows, at < count):
                        value = value.astype(jnp.bfloat16)
                        sums += value.astype(jnp.float32)
                        sides.append(value)
                    reals.append(win_ref[pl.ds(pl.multiple_of(w * BLOCK, BLOCK), BLOCK), :])
                tot_ref[...] = sums
                out_ref[rows, :] += jnp.dot(
                    jnp.concatenate(sides, axis=1),
                    jnp.concatenate(reals, axis=0),
                    preferred_element_type=jnp.float32,
                )
                return carry

            lax.fori_loop(0, (count + 3) // 4, four, 0)
            totals = jnp.sum(tot_ref[...], axis=1, keepdims=True)
            out_ref[rows, :] = totals * sim_ref[rows, :].astype(jnp.float32) - out_ref[rows, :]

    def scaled(e, k, w, rows, valid):
        p = p_ref[e * FAN + k]
        b = jnp.where(valid, b_ref[pl.ds(w, 1), :], 0.0)
        a = a_ref[rows, :]
        return p[:, :LANES] * a * b[:, :LANES], p[:, LANES:] * a * b[:, LANES:]

    def logarithmic(e, k, w, rows, valid):
        t = t_ref[e * FAN + k]
        v = v_ref[pl.ds(w, 1), :] + log_rows
        u = u_ref[rows, :]
        left, right = jnp.exp2(t[:, :LANES] + u + v[:, :LANES]), jnp.exp2(t[:, LANES:] + u + v[:, LANES:])
        return jnp.where(valid, left, 0.0), jnp.where(valid, right, 0.0)

    @pl.when(good)
    def _():
        gather(scaled)

    @pl.when(jnp.logical_not(good))
    def _():
        score_tiles(tab_ref, size_ref, sim_ref, win_ref, n_ref, t_ref, unit)
        gather(logarithmic)


def vmem():
    return pl.BlockSpec(memory_space=pltpu.VMEM)


def smem():
    return pl.BlockSpec(memory_space=pltpu.SMEM)


def shards(sim, real, pair_real, pair_count):
    replicas = lax.axis_size("rep")
    owners = lax.axis_size("blk")
    features = sim.shape[1]
    local = real.shape[0] // BLOCK
    rows_total = owners * real.shape[0]
    log_rows = math.log2(rows_total)
    unit = LOG2E / EPS / features
    mine = lax.axis_index("blk")
    rep = lax.axis_index("rep")
    fan = pair_real.shape[1]
    group = pair_real // local - mine
    group = jnp.clip(jnp.where(mine % 2 == 0, group + 1, 1 - group), 0, 2)
    table = group * local + pair_real % local
    tiles = 2 * fan
    window = 3 * local
    active = jnp.arange(fan)[None, :] < pair_count[:, None]
    ids = jnp.arange(tiles, dtype=jnp.int32)
    place = jnp.where(active, table // local, 3).reshape(-1)
    rank = jnp.sum((place * tiles + ids)[None, :] < (place * tiles + ids)[:, None], 1)
    order = jnp.sum(jnp.where(rank[:, None] == ids[None, :], ids[:, None], 0), 0)
    bounds = jnp.sum(place[:, None] < jnp.arange(4)[None, :], 0).astype(jnp.int32)
    way = 1 - 2 * (mine % 2)
    quarters = (rep + replicas + jnp.array([0, -1, 1, 2], jnp.int32) * way) % replicas
    sizes = jnp.concatenate([bounds, quarters, pair_count])
    hits = (table[:, :, None] == jnp.arange(window)) & active[:, :, None]
    used = jnp.broadcast_to(jnp.any(hits, (0, 1))[:, None], (window, BLOCK)).astype(jnp.float32)

    own = real
    first = rep_spin(own, 1)
    second = rep_spin(own, -1)
    chip_own = chip_swap(own)
    core_own = core_swap(own)
    first, second, chip_own, core_own, table, order, sizes, used = lax.optimization_barrier(
        (first, second, chip_own, core_own, table, order, sizes, used)
    )
    far = rep_spin(first, 1)
    near = jnp.stack([first, second])
    groups = {
        1: (own, near, far),
        2: (core_own, core_swap(near), core_swap(far)),
        0: (chip_own, chip_swap(near), chip_swap(far)),
    }
    sim_norm = jnp.sum(jnp.square(sim.astype(jnp.float32)), -1) * unit

    stats_shape = jax.ShapeDtypeStruct((window, BLOCK), jnp.float32)
    potentials = (2 * BLOCK, LANES)
    column = jax.ShapeDtypeStruct(potentials, jnp.float32)
    sim_rows = pltpu.with_memory_space_constraint(sim, pltpu.HBM)
    groups[1] = (pltpu.with_memory_space_constraint(own, pltpu.HBM), near, far)
    plans = pltpu.VMEM((tiles, BLOCK, BLOCK), jnp.float32)
    rows_of = pltpu.VMEM((window, BLOCK), jnp.float32)
    sums_of = pltpu.VMEM((window * 8, BLOCK), jnp.float32)
    held_sim = pltpu.VMEM(sim.shape, sim.dtype)
    col = pltpu.VMEM(potentials, jnp.float32)
    held = []
    for group in (1, 2, 0):
        last = group == 0
        found = pl.pallas_call(
            functools.partial(group_kernel, group, log_rows, unit),
            out_shape=[
                plans,
                pltpu.VMEM((window * BLOCK, features), jnp.bfloat16),
                column,
                jax.ShapeDtypeStruct((window * 8, BLOCK), jnp.float32),
                column,
            ]
            + [stats_shape] * last,
            in_specs=[smem()] * 3
            + [pl.BlockSpec(memory_space=pltpu.HBM)]
            + [pl.BlockSpec(memory_space=pltpu.HBM if group == 1 else pl.ANY)]
            + [pl.BlockSpec(memory_space=pl.ANY)] * 2
            + [vmem()] * (last + len(held)),
            out_specs=[vmem()] * (5 + last),
            input_output_aliases={7 + last + i: i for i in range(len(held))},
            scratch_shapes=[col, sums_of, plans, col, rows_of] * last + [held_sim, pltpu.SemaphoreType.DMA((5,))],
            compiler_params=pltpu.CompilerParams(vmem_limit_bytes=(16 if last else 6) * MIB),
            cost_estimate=pl.CostEstimate(flops=10**9, bytes_accessed=8 * MIB, transcendentals=0),
        )(table, order, sizes, sim_rows, *groups[group], *[used] * last, *held)
        held = [pltpu.with_memory_space_constraint(value, pltpu.VMEM) for value in found[:2]] + list(found[2:5])
    plan, window_rows, peaks, norms, _ = held
    stats_out = found[5]

    for sweep in range(ITERS):
        if sweep:
            last = sweep == ITERS - 1
            found = pl.pallas_call(
                functools.partial(sweep_kernel, last, log_rows, unit),
                out_shape=[stats_shape] + [column, jax.ShapeDtypeStruct((2, BLOCK), jnp.float32)] * last,
                in_specs=[smem()] * 2 + [vmem()] * 9 + [pl.BlockSpec(memory_space=pltpu.HBM)],
                out_specs=[vmem()] * (1 + 2 * last),
                scratch_shapes=[col] * (not last)
                + [rows_of, rows_of, col, sums_of, plans, held_sim, pltpu.SemaphoreType.DMA],
                compiler_params=pltpu.CompilerParams(vmem_limit_bytes=14 * MIB),
            )(table, sizes, *around, used, peaks, norms, plan, window_rows, sim_rows)
            stats_out = found[0]
        own_sum = log_add(stats_out[local : 2 * local], core_swap(stats_out[2 * local :]))
        chip = chip_swap(jnp.concatenate([own_sum, stats_out[:local]]))
        own_sum, chip_sum = log_add(own_sum, chip[local:]), log_add(stats_out[:local], chip[:local])
        merged = jnp.concatenate([chip_sum, own_sum, core_swap(own_sum)])
        around = (merged, rep_shift(merged, 1), rep_shift(merged, -1), rep_shift(merged, 2))

    sim_pot, sim_row = found[1:]
    back = EPS / LOG2E
    pull, real_out = pl.pallas_call(
        functools.partial(pull_kernel, log_rows, back, unit),
        out_shape=[
            jax.ShapeDtypeStruct(sim.shape, jnp.float32),
            jax.ShapeDtypeStruct((2 * local, LANES), jnp.float32),
        ],
        in_specs=[smem()] * 2 + [vmem()] * 11,
        out_specs=[vmem()] * 2,
        scratch_shapes=[rows_of, rows_of, col, pltpu.VMEM((BLOCK, LANES), jnp.float32), plans],
        compiler_params=pltpu.CompilerParams(vmem_limit_bytes=16 * MIB),
    )(table, sizes, *around, used, peaks, norms, plan, sim_pot, sim, window_rows)
    sim_out = (sim_row.reshape(-1) + sim_norm) * back
    return (pull, sim_out, real_out.reshape(-1))


def solution(mesh):
    in_specs = (
        P(("blk", "rep"), None),
        P("blk", "rep"),
        P(("blk", "rep"), None),
        P(("blk", "rep")),
    )
    out_specs = (P(("blk", "rep"), None), P(("blk", "rep")), P("blk"))
    return jax.shard_map(shards, mesh=mesh, in_specs=in_specs, out_specs=out_specs, check_vma=False)
```

```python
import functools
import math

import jax
import jax.numpy as jnp
from jax import lax
from jax.experimental import pallas as pl
from jax.experimental.pallas import tpu as pltpu
from jax.sharding import PartitionSpec as P

BLOCK = 256
ITERS = 3
EPS = 0.05
NEG = -1e30
LOG2E = math.log2(math.e)
LANES = 128
FAN = 16
LEAST, MOST = 2.0**-40, 2.0**40
HALF_NEG = -5e29
MIB = 1024 * 1024


def log_add(a, b):
    high = jnp.maximum(a, b)
    return high + jnp.log2(jnp.exp2(a - high) + jnp.exp2(b - high))


def across(index, owners):
    other = ((index + 1) ^ 1) - 1
    return other if 0 <= other < owners else index


def core_swap(value):
    owners = lax.axis_size("blk")
    return lax.ppermute(value, "blk", [(i, i ^ 1) for i in range(owners)])


def chip_swap(value):
    owners = lax.axis_size("blk")
    return lax.ppermute(value, "blk", [(i, across(i, owners)) for i in range(owners)])


def rep_flip(value, mask):
    count = lax.axis_size("rep")
    return lax.ppermute(value, "rep", [(i, i ^ mask) for i in range(count)])


def rep_turn(value, masks):
    owners, count = lax.axis_size("blk"), lax.axis_size("rep")
    pairs = []
    for owner in range(owners):
        pairs += [(owner * count + i, owner * count + (i ^ masks[owner % 2])) for i in range(count)]
    return lax.ppermute(value, ("blk", "rep"), pairs)


def row_pass(tab_ref, size_ref, t_ref, v_ref, u_ref, log_rows):
    part = 128
    for e in range(2):
        count = size_ref[8 + e]
        for c in range(BLOCK // part):
            rows = slice(c * part, (c + 1) * part)

            def scores(k):
                return t_ref[e * 16 + k, rows, :] + v_ref[pl.ds(tab_ref[e, k], 1), :]

            def peak(k, high):
                t = scores(k)
                return jnp.maximum(high, jnp.maximum(t[:, :LANES], t[:, LANES:]))

            high = lax.fori_loop(0, count, peak, jnp.full((part, LANES), NEG, jnp.float32))
            high = jnp.broadcast_to(jnp.max(high, axis=1, keepdims=True), (part, LANES))

            def total(k, acc):
                t = scores(k)
                return acc + jnp.exp2(t[:, :LANES] - high) + jnp.exp2(t[:, LANES:] - high)

            acc = lax.fori_loop(0, count, total, jnp.zeros((part, LANES), jnp.float32))
            acc = jnp.broadcast_to(jnp.sum(acc, axis=1, keepdims=True), (part, LANES))
            u_ref[e * BLOCK + c * part : e * BLOCK + (c + 1) * part, :] = (
                -(high + jnp.log2(acc)) - log_rows
            )


def column_pass(tab_ref, size_ref, t_ref, u_ref, l_ref):
    window = l_ref.shape[0]
    row_ids = lax.broadcasted_iota(jnp.int32, (window, LANES), 0)
    stats = []
    for e in range(2):

        def tile(k, carry):
            here = row_ids == tab_ref[e, k]
            after = []
            for half in range(2):
                lanes = slice(half * LANES, (half + 1) * LANES)
                highs, sums = carry[half]
                t = t_ref[e * 16 + k, :, lanes] + u_ref[e * BLOCK : (e + 1) * BLOCK, :]
                high = jnp.max(t, axis=0, keepdims=True)
                total = jnp.sum(jnp.exp2(t - high), axis=0, keepdims=True)
                after.append((jnp.where(here, high, highs), jnp.where(here, total, sums)))
            return tuple(after)

        start = (jnp.full((window, LANES), NEG, jnp.float32), jnp.ones((window, LANES), jnp.float32))
        found = lax.fori_loop(0, size_ref[8 + e], tile, (start, start))
        stats.append([high + jnp.log2(total) for high, total in found])
    for half in range(2):
        l_ref[:, half * LANES : (half + 1) * LANES] = log_add(stats[0][half], stats[1][half])


def lanes_of(column, rows):
    return jnp.broadcast_to(column, (rows, LANES))


def scaled_columns(tab_ref, size_ref, p_ref, a_ref, c_ref):
    c_ref[...] = jnp.zeros(c_ref.shape, jnp.float32)
    for e in range(2):
        count = size_ref[8 + e]

        def pair(i, carry):
            a = a_ref[e * BLOCK : (e + 1) * BLOCK, :]
            for at in (2 * i, 2 * i + 1):
                k = jnp.minimum(at, count - 1)
                p = p_ref[e * FAN + k]
                rows = pl.ds(pl.multiple_of(tab_ref[e, k] * 8, 8), 8)
                for half in range(2):
                    lanes = slice(half * LANES, (half + 1) * LANES)
                    terms = jnp.sum((p[:, lanes] * a).reshape(BLOCK // 8, 8, LANES), axis=0)
                    c_ref[rows, lanes] += jnp.where(at < count, terms, 0.0)
            return carry

        lax.fori_loop(0, (count + 1) // 2, pair, 0)
    window = c_ref.shape[0] // 8
    return jnp.sum(c_ref[...].reshape(window, 8, BLOCK), axis=1)


def scaled_rows(tab_ref, size_ref, p_ref, b_ref, r_ref):
    for e in range(2):
        count = size_ref[8 + e]

        def pair(i, acc):
            for at in (2 * i, 2 * i + 1):
                k = jnp.minimum(at, count - 1)
                p = p_ref[e * FAN + k]
                b = jnp.where(at < count, b_ref[pl.ds(tab_ref[e, k], 1), :], 0.0)
                acc = acc + p[:, :LANES] * b[:, :LANES] + p[:, LANES:] * b[:, LANES:]
            return acc

        acc = lax.fori_loop(0, (count + 1) // 2, pair, jnp.zeros((BLOCK, LANES), jnp.float32))
        r_ref[e * BLOCK : (e + 1) * BLOCK, :] = lanes_of(jnp.sum(acc, axis=1, keepdims=True), BLOCK)


def within(value):
    return jnp.logical_and(jnp.min(value) >= LEAST, jnp.max(value) <= MOST)


def score_tile(sim_ref, win_ref, n_ref, block, w, unit):
    dots = lax.dot_general(
        sim_ref[block, :],
        win_ref[pl.ds(pl.multiple_of(w * BLOCK, BLOCK), BLOCK), :],
        (((1,), (1,)), ((), ())),
        preferred_element_type=jnp.float32,
    )
    return dots * (2.0 * unit) - n_ref[pl.ds(w * 8, 1), :]


def score_tiles(tab_ref, size_ref, sim_ref, win_ref, n_ref, t_ref, unit):
    for e in range(2):

        def tile(k, carry):
            block = slice(e * BLOCK, (e + 1) * BLOCK)
            t_ref[e * FAN + k] = score_tile(sim_ref, win_ref, n_ref, block, tab_ref[e, k], unit)
            return carry

        lax.fori_loop(0, size_ref[8 + e], tile, 0)


def group_kernel(group, log_rows, unit, tab_ref, order_ref, size_ref, sim_hbm, own_ref, near_ref, far_ref, *refs):
    last = group == 0
    if last:
        used_ref, refs = refs[0], refs[1:]
    if group != 1:
        refs = refs[5:]
    p_ref, win_ref, m_ref, n_ref, r_ref = refs[:5]
    refs = refs[5:]
    sim_ref, sems = refs[-2:]
    rows = own_ref.shape[0]
    local = rows // BLOCK
    sources = [own_ref, near_ref.at[0], near_ref.at[1], far_ref]
    copies = [pltpu.make_async_copy(sim_hbm, sim_ref, sems.at[4])]
    for i, source in enumerate(sources):
        at = i if group == 1 else (0, 2, 1, 3)[i]
        q = pl.multiple_of(size_ref[4 + at] * LANES, LANES)
        target = win_ref.at[pl.ds(group * rows, rows), pl.ds(q, LANES)]
        copies.append(pltpu.make_async_copy(source, target, sems.at[i]))
    for copy in copies:
        copy.start()
    for copy in copies:
        copy.wait()

    ones = jnp.ones((8, LANES), jnp.bfloat16)

    def norms(i, carry):
        start = pl.multiple_of((group * local + i) * BLOCK, BLOCK)
        y = win_ref[pl.ds(start, BLOCK), :].astype(jnp.float32)
        y = y * y
        part = (y[:, :LANES] + y[:, LANES : 2 * LANES]) + (y[:, 2 * LANES : 3 * LANES] + y[:, 3 * LANES :])
        total = jnp.zeros((8, BLOCK), jnp.float32)
        for _ in range(3):
            piece = part.astype(jnp.bfloat16)
            part = part - piece.astype(jnp.float32)
            total = total + lax.dot_general(
                ones, piece, (((1,), (1,)), ((), ())), preferred_element_type=jnp.float32
            )
        n_ref[pl.ds(pl.multiple_of((group * local + i) * 8, 8), 8), :] = total * unit
        return carry

    lax.fori_loop(0, local, norms, 0, unroll=4)
    if group == 1:
        r_ref[...] = jnp.zeros(r_ref.shape, jnp.float32)
        for e in range(2):
            block = slice(e * BLOCK, (e + 1) * BLOCK)
            t = score_tile(sim_ref, win_ref, n_ref, block, tab_ref[e, 0], unit)
            high = jnp.maximum(t[:, :LANES], t[:, LANES:])
            m_ref[block, :] = lanes_of(jnp.max(high, axis=1, keepdims=True), BLOCK)
    first, end = size_ref[group], size_ref[group + 1]

    def build(at, valid):
        slot = order_ref[at]
        e = slot // FAN
        block = pl.ds(pl.multiple_of(e * BLOCK, BLOCK), BLOCK)
        t = score_tile(sim_ref, win_ref, n_ref, block, tab_ref[e, slot % FAN], unit)
        offset = m_ref[block, :]
        left = jnp.exp2(t[:, :LANES] - offset)
        right = jnp.exp2(t[:, LANES:] - offset)
        p_ref[slot, :, :LANES] = left
        p_ref[slot, :, LANES:] = right
        both = left + right
        r_ref[block, :] += both if valid is None else jnp.where(valid, both, 0.0)

    def four(i, carry):
        at = first + 4 * i
        build(at, None)
        build(jnp.minimum(at + 1, end - 1), at + 1 < end)
        build(jnp.minimum(at + 2, end - 1), at + 2 < end)
        build(jnp.minimum(at + 3, end - 1), at + 3 < end)
        return carry

    lax.fori_loop(0, (end - first + 3) // 4, four, 0)

    if last:
        l_ref, a_ref, c_ref, t_ref, u_ref, v_ref = refs[:6]
        good = True
        for e in range(2):
            block = slice(e * BLOCK, (e + 1) * BLOCK)
            total = lanes_of(jnp.sum(r_ref[block, :], axis=1, keepdims=True), BLOCK)
            a_ref[block, :] = 1.0 / total
            good = jnp.logical_and(good, within(total))
        good = columns_out(tab_ref, size_ref, p_ref, a_ref, used_ref, c_ref, l_ref, log_rows, good)

        @pl.when(jnp.logical_not(good))
        def _():
            v_ref[...] = jnp.zeros(v_ref.shape, jnp.float32)
            score_tiles(tab_ref, size_ref, sim_ref, win_ref, n_ref, t_ref, unit)
            row_pass(tab_ref, size_ref, t_ref, v_ref, u_ref, log_rows)
            column_pass(tab_ref, size_ref, t_ref, u_ref, l_ref)


def columns_out(tab_ref, size_ref, p_ref, a_ref, used_ref, c_ref, l_ref, log_rows, good):
    used = used_ref[...] > 0.0
    total = jnp.where(used, scaled_columns(tab_ref, size_ref, p_ref, a_ref, c_ref), 1.0)
    l_ref[...] = jnp.where(used, jnp.log2(total) - log_rows, NEG)
    return jnp.logical_and(good, within(total))


def joined(stats_refs, log_rows):
    a, b, c, d = [ref[...] for ref in stats_refs]
    high = jnp.maximum(jnp.maximum(a, b), jnp.maximum(c, d))
    total = jnp.exp2(a - high) + jnp.exp2(b - high) + jnp.exp2(c - high) + jnp.exp2(d - high)
    return jnp.where(high > HALF_NEG, -(high + jnp.log2(total)) - log_rows, 0.0)


def sweep_kernel(
    last, log_rows, unit, tab_ref, size_ref, s0, s1, s2, s3, used_ref, m_ref, n_ref, p_ref, win_ref, sim_hbm, *refs
):
    l_ref, refs = refs[0], refs[1:]
    if last:
        u_ref, row_ref, *refs = refs
        v_ref, b_ref, a_ref, c_ref, t_ref, sim_ref, sem = refs
    else:
        u_ref, v_ref, b_ref, a_ref, c_ref, t_ref, sim_ref, sem = refs
    v = jnp.where(used_ref[...] > 0.0, joined((s0, s1, s2, s3), log_rows), 0.0)
    v_ref[...] = v
    b = jnp.exp2(v)
    b_ref[...] = b
    scaled_rows(tab_ref, size_ref, p_ref, b_ref, a_ref)
    totals = a_ref[...]
    good = jnp.logical_and(within(b), within(totals))
    if last:
        u_ref[...] = -(m_ref[...] + jnp.log2(totals)) - log_rows
    a_ref[...] = 1.0 / totals
    good = columns_out(tab_ref, size_ref, p_ref, a_ref, used_ref, c_ref, l_ref, log_rows, good)

    @pl.when(jnp.logical_not(good))
    def _():
        copy = pltpu.make_async_copy(sim_hbm, sim_ref, sem)
        copy.start()
        copy.wait()
        score_tiles(tab_ref, size_ref, sim_ref, win_ref, n_ref, t_ref, unit)
        row_pass(tab_ref, size_ref, t_ref, v_ref, u_ref, log_rows)
        column_pass(tab_ref, size_ref, t_ref, u_ref, l_ref)

    if last:
        for e in range(2):
            row_ref[e : e + 1, :] = jnp.transpose(u_ref[e * BLOCK : (e + 1) * BLOCK, :])[0:1, :]


def pull_kernel(
    log_rows, back, unit, tab_ref, size_ref, s0, s1, s2, s3, used_ref, m_ref, n_ref, p_ref, u_ref, sim_ref, win_ref,
    out_ref, real_ref, v_ref, b_ref, a_ref, tot_ref, t_ref
):
    potential = joined((s0, s1, s2, s3), log_rows)
    v_ref[...] = potential
    own = real_ref.shape[0] // 2
    for i in range(own):
        for half in range(2):
            real_ref[2 * i + half : 2 * i + half + 1, :] = (
                potential[own + i : own + i + 1, half * LANES : (half + 1) * LANES] * back
            )
    v = jnp.where(used_ref[...] > 0.0, potential, 0.0)
    b = jnp.exp2(v)
    b_ref[...] = b
    a = jnp.exp2(u_ref[...] + m_ref[...] + log_rows)
    a_ref[...] = a
    good = jnp.logical_and(within(b), within(a))

    def gather(weights):
        for e in range(2):
            rows = slice(e * BLOCK, (e + 1) * BLOCK)
            count = size_ref[8 + e]
            out_ref[rows, :] = jnp.zeros((BLOCK, out_ref.shape[1]), jnp.float32)
            tot_ref[...] = jnp.zeros(tot_ref.shape, jnp.float32)

            def four(i, carry):
                sides, reals = [], []
                sums = tot_ref[...]
                for at in (4 * i, 4 * i + 1, 4 * i + 2, 4 * i + 3):
                    k = jnp.minimum(at, count - 1)
                    w = tab_ref[e, k]
                    for value in weights(e, k, w, rows, at < count):
                        value = value.astype(jnp.bfloat16)
                        sums += value.astype(jnp.float32)
                        sides.append(value)
                    reals.append(win_ref[pl.ds(pl.multiple_of(w * BLOCK, BLOCK), BLOCK), :])
                tot_ref[...] = sums
                out_ref[rows, :] += jnp.dot(
                    jnp.concatenate(sides, axis=1),
                    jnp.concatenate(reals, axis=0),
                    preferred_element_type=jnp.float32,
                )
                return carry

            lax.fori_loop(0, (count + 3) // 4, four, 0)
            totals = jnp.sum(tot_ref[...], axis=1, keepdims=True)
            out_ref[rows, :] = totals * sim_ref[rows, :].astype(jnp.float32) - out_ref[rows, :]

    def scaled(e, k, w, rows, valid):
        p = p_ref[e * FAN + k]
        b = jnp.where(valid, b_ref[pl.ds(w, 1), :], 0.0)
        a = a_ref[rows, :]
        return p[:, :LANES] * a * b[:, :LANES], p[:, LANES:] * a * b[:, LANES:]

    def logarithmic(e, k, w, rows, valid):
        t = t_ref[e * FAN + k]
        v = v_ref[pl.ds(w, 1), :] + log_rows
        u = u_ref[rows, :]
        left, right = jnp.exp2(t[:, :LANES] + u + v[:, :LANES]), jnp.exp2(t[:, LANES:] + u + v[:, LANES:])
        return jnp.where(valid, left, 0.0), jnp.where(valid, right, 0.0)

    @pl.when(good)
    def _():
        gather(scaled)

    @pl.when(jnp.logical_not(good))
    def _():
        score_tiles(tab_ref, size_ref, sim_ref, win_ref, n_ref, t_ref, unit)
        gather(logarithmic)


def vmem():
    return pl.BlockSpec(memory_space=pltpu.VMEM)


def smem():
    return pl.BlockSpec(memory_space=pltpu.SMEM)


def shards(sim, real, pair_real, pair_count):
    owners = lax.axis_size("blk")
    features = sim.shape[1]
    local = real.shape[0] // BLOCK
    rows_total = owners * real.shape[0]
    log_rows = math.log2(rows_total)
    unit = LOG2E / EPS / features
    mine = lax.axis_index("blk")
    rep = lax.axis_index("rep")
    fan = pair_real.shape[1]
    group = pair_real // local - mine
    group = jnp.clip(jnp.where(mine % 2 == 0, group + 1, 1 - group), 0, 2)
    table = group * local + pair_real % local
    tiles = 2 * fan
    window = 3 * local
    active = jnp.arange(fan)[None, :] < pair_count[:, None]
    ids = jnp.arange(tiles, dtype=jnp.int32)
    place = jnp.where(active, table // local, 3).reshape(-1)
    rank = jnp.sum((place * tiles + ids)[None, :] < (place * tiles + ids)[:, None], 1)
    order = jnp.sum(jnp.where(rank[:, None] == ids[None, :], ids[:, None], 0), 0)
    bounds = jnp.sum(place[:, None] < jnp.arange(4)[None, :], 0).astype(jnp.int32)
    masks = jnp.where(mine % 2 == 0, jnp.array([0, 1, 3, 2], jnp.int32), jnp.array([0, 3, 1, 2], jnp.int32))
    quarters = rep ^ masks
    sizes = jnp.concatenate([bounds, quarters, pair_count])
    hits = (table[:, :, None] == jnp.arange(window)) & active[:, :, None]
    used = jnp.broadcast_to(jnp.any(hits, (0, 1))[:, None], (window, BLOCK)).astype(jnp.float32)

    own = real
    first = rep_turn(own, (1, 3))
    second = rep_turn(own, (3, 1))
    chip_own = chip_swap(own)
    core_own = core_swap(own)
    first, second, chip_own, core_own, table, order, sizes, used = lax.optimization_barrier(
        (first, second, chip_own, core_own, table, order, sizes, used)
    )
    far = rep_turn(first, (3, 1))
    near = jnp.stack([first, second])
    groups = {
        1: (own, near, far),
        2: (core_own, core_swap(near), core_swap(far)),
        0: (chip_own, chip_swap(near), chip_swap(far)),
    }
    sim_norm = jnp.sum(jnp.square(sim.astype(jnp.float32)), -1) * unit

    stats_shape = jax.ShapeDtypeStruct((window, BLOCK), jnp.float32)
    potentials = (2 * BLOCK, LANES)
    column = jax.ShapeDtypeStruct(potentials, jnp.float32)
    sim_rows = pltpu.with_memory_space_constraint(sim, pltpu.HBM)
    groups[1] = (pltpu.with_memory_space_constraint(own, pltpu.HBM), near, far)
    plans = pltpu.VMEM((tiles, BLOCK, BLOCK), jnp.float32)
    rows_of = pltpu.VMEM((window, BLOCK), jnp.float32)
    sums_of = pltpu.VMEM((window * 8, BLOCK), jnp.float32)
    held_sim = pltpu.VMEM(sim.shape, sim.dtype)
    col = pltpu.VMEM(potentials, jnp.float32)
    held = []
    for group in (1, 2, 0):
        last = group == 0
        found = pl.pallas_call(
            functools.partial(group_kernel, group, log_rows, unit),
            out_shape=[
                plans,
                pltpu.VMEM((window * BLOCK, features), jnp.bfloat16),
                column,
                jax.ShapeDtypeStruct((window * 8, BLOCK), jnp.float32),
                column,
            ]
            + [stats_shape] * last,
            in_specs=[smem()] * 3
            + [pl.BlockSpec(memory_space=pltpu.HBM)]
            + [pl.BlockSpec(memory_space=pltpu.HBM if group == 1 else pl.ANY)]
            + [pl.BlockSpec(memory_space=pl.ANY)] * 2
            + [vmem()] * (last + len(held)),
            out_specs=[vmem()] * (5 + last),
            input_output_aliases={7 + last + i: i for i in range(len(held))},
            scratch_shapes=[col, sums_of, plans, col, rows_of] * last + [held_sim, pltpu.SemaphoreType.DMA((5,))],
            compiler_params=pltpu.CompilerParams(vmem_limit_bytes=(16 if last else 6) * MIB),
            cost_estimate=pl.CostEstimate(flops=10**9, bytes_accessed=8 * MIB, transcendentals=0),
        )(table, order, sizes, sim_rows, *groups[group], *[used] * last, *held)
        held = [pltpu.with_memory_space_constraint(value, pltpu.VMEM) for value in found[:2]] + list(found[2:5])
    plan, window_rows, peaks, norms, _ = held
    stats_out = found[5]

    for sweep in range(ITERS):
        if sweep:
            last = sweep == ITERS - 1
            found = pl.pallas_call(
                functools.partial(sweep_kernel, last, log_rows, unit),
                out_shape=[stats_shape] + [column, jax.ShapeDtypeStruct((2, BLOCK), jnp.float32)] * last,
                in_specs=[smem()] * 2 + [vmem()] * 9 + [pl.BlockSpec(memory_space=pltpu.HBM)],
                out_specs=[vmem()] * (1 + 2 * last),
                scratch_shapes=[col] * (not last)
                + [rows_of, rows_of, col, sums_of, plans, held_sim, pltpu.SemaphoreType.DMA],
                compiler_params=pltpu.CompilerParams(vmem_limit_bytes=14 * MIB),
            )(table, sizes, *around, used, peaks, norms, plan, window_rows, sim_rows)
            stats_out = found[0]
        own_sum = log_add(stats_out[local : 2 * local], core_swap(stats_out[2 * local :]))
        chip = chip_swap(jnp.concatenate([own_sum, stats_out[:local]]))
        own_sum, chip_sum = log_add(own_sum, chip[local:]), log_add(stats_out[:local], chip[:local])
        merged = jnp.concatenate([chip_sum, own_sum, core_swap(own_sum)])
        around = (merged, rep_flip(merged, 1), rep_flip(merged, 3), rep_flip(merged, 2))

    sim_pot, sim_row = found[1:]
    back = EPS / LOG2E
    pull, real_out = pl.pallas_call(
        functools.partial(pull_kernel, log_rows, back, unit),
        out_shape=[
            jax.ShapeDtypeStruct(sim.shape, jnp.float32),
            jax.ShapeDtypeStruct((2 * local, LANES), jnp.float32),
        ],
        in_specs=[smem()] * 2 + [vmem()] * 11,
        out_specs=[vmem()] * 2,
        scratch_shapes=[rows_of, rows_of, col, pltpu.VMEM((BLOCK, LANES), jnp.float32), plans],
        compiler_params=pltpu.CompilerParams(vmem_limit_bytes=16 * MIB),
    )(table, sizes, *around, used, peaks, norms, plan, sim_pot, sim, window_rows)
    sim_out = (sim_row.reshape(-1) + sim_norm) * back
    return (pull, sim_out, real_out.reshape(-1))


def solution(mesh):
    in_specs = (
        P(("blk", "rep"), None),
        P("blk", "rep"),
        P(("blk", "rep"), None),
        P(("blk", "rep")),
    )
    out_specs = (P(("blk", "rep"), None), P(("blk", "rep")), P("blk"))
    return jax.shard_map(shards, mesh=mesh, in_specs=in_specs, out_specs=out_specs, check_vma=False)
```

```python
import functools
import math

import jax
import jax.numpy as jnp
from jax import lax
from jax.experimental import pallas as pl
from jax.experimental.pallas import tpu as pltpu
from jax.sharding import PartitionSpec as P

BLOCK = 256
ITERS = 3
EPS = 0.05
NEG = -1e30
LOG2E = math.log2(math.e)
LANES = 128
FAN = 16
LEAST, MOST = 2.0**-40, 2.0**40
HALF_NEG = -5e29
MIB = 1024 * 1024


def log_add(a, b):
    high = jnp.maximum(a, b)
    return high + jnp.log2(jnp.exp2(a - high) + jnp.exp2(b - high))


def across(index, owners):
    other = ((index + 1) ^ 1) - 1
    return other if 0 <= other < owners else index


def core_swap(value):
    owners = lax.axis_size("blk")
    return lax.ppermute(value, "blk", [(i, i ^ 1) for i in range(owners)])


def chip_swap(value):
    owners = lax.axis_size("blk")
    return lax.ppermute(value, "blk", [(i, across(i, owners)) for i in range(owners)])


def rep_flip(value, mask):
    count = lax.axis_size("rep")
    return lax.ppermute(value, "rep", [(i, i ^ mask) for i in range(count)])


def rep_turn(value, masks):
    owners, count = lax.axis_size("blk"), lax.axis_size("rep")
    pairs = []
    for owner in range(owners):
        pairs += [(owner * count + i, owner * count + (i ^ masks[owner % 2])) for i in range(count)]
    return lax.ppermute(value, ("blk", "rep"), pairs)


def row_pass(tab_ref, size_ref, t_ref, v_ref, u_ref, log_rows):
    part = 128
    for e in range(2):
        count = size_ref[8 + e]
        for c in range(BLOCK // part):
            rows = slice(c * part, (c + 1) * part)

            def scores(k):
                return t_ref[e * 16 + k, rows, :] + v_ref[pl.ds(tab_ref[e, k], 1), :]

            def peak(k, high):
                t = scores(k)
                return jnp.maximum(high, jnp.maximum(t[:, :LANES], t[:, LANES:]))

            high = lax.fori_loop(0, count, peak, jnp.full((part, LANES), NEG, jnp.float32))
            high = jnp.broadcast_to(jnp.max(high, axis=1, keepdims=True), (part, LANES))

            def total(k, acc):
                t = scores(k)
                return acc + jnp.exp2(t[:, :LANES] - high) + jnp.exp2(t[:, LANES:] - high)

            acc = lax.fori_loop(0, count, total, jnp.zeros((part, LANES), jnp.float32))
            acc = jnp.broadcast_to(jnp.sum(acc, axis=1, keepdims=True), (part, LANES))
            u_ref[e * BLOCK + c * part : e * BLOCK + (c + 1) * part, :] = (
                -(high + jnp.log2(acc)) - log_rows
            )


def column_pass(tab_ref, size_ref, t_ref, u_ref, l_ref):
    window = l_ref.shape[0]
    row_ids = lax.broadcasted_iota(jnp.int32, (window, LANES), 0)
    stats = []
    for e in range(2):

        def tile(k, carry):
            here = row_ids == tab_ref[e, k]
            after = []
            for half in range(2):
                lanes = slice(half * LANES, (half + 1) * LANES)
                highs, sums = carry[half]
                t = t_ref[e * 16 + k, :, lanes] + u_ref[e * BLOCK : (e + 1) * BLOCK, :]
                high = jnp.max(t, axis=0, keepdims=True)
                total = jnp.sum(jnp.exp2(t - high), axis=0, keepdims=True)
                after.append((jnp.where(here, high, highs), jnp.where(here, total, sums)))
            return tuple(after)

        start = (jnp.full((window, LANES), NEG, jnp.float32), jnp.ones((window, LANES), jnp.float32))
        found = lax.fori_loop(0, size_ref[8 + e], tile, (start, start))
        stats.append([high + jnp.log2(total) for high, total in found])
    for half in range(2):
        l_ref[:, half * LANES : (half + 1) * LANES] = log_add(stats[0][half], stats[1][half])


def lanes_of(column, rows):
    return jnp.broadcast_to(column, (rows, LANES))


def scaled_columns(tab_ref, size_ref, p_ref, a_ref, c_ref):
    c_ref[...] = jnp.zeros(c_ref.shape, jnp.float32)
    for e in range(2):
        count = size_ref[8 + e]

        def four(i, carry):
            a = a_ref[e * BLOCK : (e + 1) * BLOCK, :]
            for at in (4 * i, 4 * i + 1, 4 * i + 2, 4 * i + 3):
                k = jnp.minimum(at, count - 1)
                p = p_ref[e * FAN + k]
                rows = pl.ds(pl.multiple_of(tab_ref[e, k] * 8, 8), 8)
                for half in range(2):
                    lanes = slice(half * LANES, (half + 1) * LANES)
                    terms = jnp.sum((p[:, lanes] * a).reshape(BLOCK // 8, 8, LANES), axis=0)
                    c_ref[rows, lanes] += jnp.where(at < count, terms, 0.0)
            return carry

        lax.fori_loop(0, (count + 3) // 4, four, 0)
    window = c_ref.shape[0] // 8
    return jnp.sum(c_ref[...].reshape(window, 8, BLOCK), axis=1)


def scaled_rows(tab_ref, size_ref, p_ref, b_ref, r_ref):
    for e in range(2):
        count = size_ref[8 + e]

        def four(i, acc):
            for at in (4 * i, 4 * i + 1, 4 * i + 2, 4 * i + 3):
                k = jnp.minimum(at, count - 1)
                p = p_ref[e * FAN + k]
                b = jnp.where(at < count, b_ref[pl.ds(tab_ref[e, k], 1), :], 0.0)
                acc = acc + p[:, :LANES] * b[:, :LANES] + p[:, LANES:] * b[:, LANES:]
            return acc

        acc = lax.fori_loop(0, (count + 3) // 4, four, jnp.zeros((BLOCK, LANES), jnp.float32))
        r_ref[e * BLOCK : (e + 1) * BLOCK, :] = lanes_of(jnp.sum(acc, axis=1, keepdims=True), BLOCK)


def within(value):
    return jnp.logical_and(jnp.min(value) >= LEAST, jnp.max(value) <= MOST)


def score_tile(sim_ref, win_ref, n_ref, block, w, unit):
    dots = lax.dot_general(
        sim_ref[block, :],
        win_ref[pl.ds(pl.multiple_of(w * BLOCK, BLOCK), BLOCK), :],
        (((1,), (1,)), ((), ())),
        preferred_element_type=jnp.float32,
    )
    return dots * (2.0 * unit) - n_ref[pl.ds(w * 8, 1), :]


def score_tiles(tab_ref, size_ref, sim_ref, win_ref, n_ref, t_ref, unit):
    for e in range(2):

        def tile(k, carry):
            block = slice(e * BLOCK, (e + 1) * BLOCK)
            t_ref[e * FAN + k] = score_tile(sim_ref, win_ref, n_ref, block, tab_ref[e, k], unit)
            return carry

        lax.fori_loop(0, size_ref[8 + e], tile, 0)


def group_kernel(group, log_rows, unit, tab_ref, order_ref, size_ref, sim_hbm, own_ref, near_ref, far_ref, *refs):
    last = group == 0
    if last:
        used_ref, refs = refs[0], refs[1:]
    if group != 1:
        refs = refs[5:]
    p_ref, win_ref, m_ref, n_ref, r_ref = refs[:5]
    refs = refs[5:]
    sim_ref, sems = refs[-2:]
    rows = own_ref.shape[0]
    local = rows // BLOCK
    sources = [own_ref, near_ref.at[0], near_ref.at[1], far_ref]
    copies = [pltpu.make_async_copy(sim_hbm, sim_ref, sems.at[4])]
    for i, source in enumerate(sources):
        at = i if group == 1 else (0, 2, 1, 3)[i]
        q = pl.multiple_of(size_ref[4 + at] * LANES, LANES)
        target = win_ref.at[pl.ds(group * rows, rows), pl.ds(q, LANES)]
        copies.append(pltpu.make_async_copy(source, target, sems.at[i]))
    for copy in copies:
        copy.start()
    for copy in copies:
        copy.wait()

    ones = jnp.ones((8, LANES), jnp.bfloat16)

    def norms(i, carry):
        start = pl.multiple_of((group * local + i) * BLOCK, BLOCK)
        y = win_ref[pl.ds(start, BLOCK), :].astype(jnp.float32)
        y = y * y
        part = (y[:, :LANES] + y[:, LANES : 2 * LANES]) + (y[:, 2 * LANES : 3 * LANES] + y[:, 3 * LANES :])
        total = jnp.zeros((8, BLOCK), jnp.float32)
        for _ in range(3):
            piece = part.astype(jnp.bfloat16)
            part = part - piece.astype(jnp.float32)
            total = total + lax.dot_general(
                ones, piece, (((1,), (1,)), ((), ())), preferred_element_type=jnp.float32
            )
        n_ref[pl.ds(pl.multiple_of((group * local + i) * 8, 8), 8), :] = total * unit
        return carry

    lax.fori_loop(0, local, norms, 0, unroll=8)
    if group == 1:
        r_ref[...] = jnp.zeros(r_ref.shape, jnp.float32)
        for e in range(2):
            block = slice(e * BLOCK, (e + 1) * BLOCK)
            t = score_tile(sim_ref, win_ref, n_ref, block, tab_ref[e, 0], unit)
            high = jnp.maximum(t[:, :LANES], t[:, LANES:])
            m_ref[block, :] = lanes_of(jnp.max(high, axis=1, keepdims=True), BLOCK)
    first, end = size_ref[group], size_ref[group + 1]

    def build(at, valid):
        slot = order_ref[at]
        e = slot // FAN
        block = pl.ds(pl.multiple_of(e * BLOCK, BLOCK), BLOCK)
        t = score_tile(sim_ref, win_ref, n_ref, block, tab_ref[e, slot % FAN], unit)
        offset = m_ref[block, :]
        left = jnp.exp2(t[:, :LANES] - offset)
        right = jnp.exp2(t[:, LANES:] - offset)
        p_ref[slot, :, :LANES] = left
        p_ref[slot, :, LANES:] = right
        both = left + right
        r_ref[block, :] += both if valid is None else jnp.where(valid, both, 0.0)

    def four(i, carry):
        at = first + 4 * i
        build(at, None)
        build(jnp.minimum(at + 1, end - 1), at + 1 < end)
        build(jnp.minimum(at + 2, end - 1), at + 2 < end)
        build(jnp.minimum(at + 3, end - 1), at + 3 < end)
        return carry

    lax.fori_loop(0, (end - first + 3) // 4, four, 0)

    if last:
        l_ref, a_ref, c_ref, t_ref, u_ref, v_ref = refs[:6]
        good = True
        for e in range(2):
            block = slice(e * BLOCK, (e + 1) * BLOCK)
            total = lanes_of(jnp.sum(r_ref[block, :], axis=1, keepdims=True), BLOCK)
            a_ref[block, :] = 1.0 / total
            good = jnp.logical_and(good, within(total))
        good = columns_out(tab_ref, size_ref, p_ref, a_ref, used_ref, c_ref, l_ref, log_rows, good)

        @pl.when(jnp.logical_not(good))
        def _():
            v_ref[...] = jnp.zeros(v_ref.shape, jnp.float32)
            score_tiles(tab_ref, size_ref, sim_ref, win_ref, n_ref, t_ref, unit)
            row_pass(tab_ref, size_ref, t_ref, v_ref, u_ref, log_rows)
            column_pass(tab_ref, size_ref, t_ref, u_ref, l_ref)


def columns_out(tab_ref, size_ref, p_ref, a_ref, used_ref, c_ref, l_ref, log_rows, good):
    used = used_ref[...] > 0.0
    total = jnp.where(used, scaled_columns(tab_ref, size_ref, p_ref, a_ref, c_ref), 1.0)
    l_ref[...] = jnp.where(used, jnp.log2(total) - log_rows, NEG)
    return jnp.logical_and(good, within(total))


def joined(stats_refs, log_rows):
    a, b, c, d = [ref[...] for ref in stats_refs]
    high = jnp.maximum(jnp.maximum(a, b), jnp.maximum(c, d))
    total = jnp.exp2(a - high) + jnp.exp2(b - high) + jnp.exp2(c - high) + jnp.exp2(d - high)
    return jnp.where(high > HALF_NEG, -(high + jnp.log2(total)) - log_rows, 0.0)


def sweep_kernel(
    last, log_rows, unit, tab_ref, size_ref, s0, s1, s2, s3, used_ref, m_ref, n_ref, p_ref, win_ref, sim_hbm, *refs
):
    l_ref, refs = refs[0], refs[1:]
    if last:
        u_ref, row_ref, *refs = refs
        v_ref, b_ref, a_ref, c_ref, t_ref, sim_ref, sem = refs
    else:
        u_ref, v_ref, b_ref, a_ref, c_ref, t_ref, sim_ref, sem = refs
    v = jnp.where(used_ref[...] > 0.0, joined((s0, s1, s2, s3), log_rows), 0.0)
    v_ref[...] = v
    b = jnp.exp2(v)
    b_ref[...] = b
    scaled_rows(tab_ref, size_ref, p_ref, b_ref, a_ref)
    totals = a_ref[...]
    good = jnp.logical_and(within(b), within(totals))
    if last:
        u_ref[...] = -(m_ref[...] + jnp.log2(totals)) - log_rows
    a_ref[...] = 1.0 / totals
    good = columns_out(tab_ref, size_ref, p_ref, a_ref, used_ref, c_ref, l_ref, log_rows, good)

    @pl.when(jnp.logical_not(good))
    def _():
        copy = pltpu.make_async_copy(sim_hbm, sim_ref, sem)
        copy.start()
        copy.wait()
        score_tiles(tab_ref, size_ref, sim_ref, win_ref, n_ref, t_ref, unit)
        row_pass(tab_ref, size_ref, t_ref, v_ref, u_ref, log_rows)
        column_pass(tab_ref, size_ref, t_ref, u_ref, l_ref)

    if last:
        for e in range(2):
            row_ref[e : e + 1, :] = jnp.transpose(u_ref[e * BLOCK : (e + 1) * BLOCK, :])[0:1, :]


def pull_kernel(
    log_rows, back, unit, tab_ref, size_ref, s0, s1, s2, s3, used_ref, m_ref, n_ref, p_ref, u_ref, sim_ref, win_ref,
    out_ref, real_ref, v_ref, b_ref, a_ref, tot_ref, t_ref
):
    potential = joined((s0, s1, s2, s3), log_rows)
    v_ref[...] = potential
    own = real_ref.shape[0] // 2
    for i in range(own):
        for half in range(2):
            real_ref[2 * i + half : 2 * i + half + 1, :] = (
                potential[own + i : own + i + 1, half * LANES : (half + 1) * LANES] * back
            )
    v = jnp.where(used_ref[...] > 0.0, potential, 0.0)
    b = jnp.exp2(v)
    b_ref[...] = b
    a = jnp.exp2(u_ref[...] + m_ref[...] + log_rows)
    a_ref[...] = a
    good = jnp.logical_and(within(b), within(a))

    def gather(weights):
        for e in range(2):
            rows = slice(e * BLOCK, (e + 1) * BLOCK)
            count = size_ref[8 + e]
            out_ref[rows, :] = jnp.zeros((BLOCK, out_ref.shape[1]), jnp.float32)
            tot_ref[...] = jnp.zeros(tot_ref.shape, jnp.float32)

            def four(i, carry):
                sides, reals = [], []
                sums = tot_ref[...]
                for at in (4 * i, 4 * i + 1, 4 * i + 2, 4 * i + 3):
                    k = jnp.minimum(at, count - 1)
                    w = tab_ref[e, k]
                    for value in weights(e, k, w, rows, at < count):
                        value = value.astype(jnp.bfloat16)
                        sums += value.astype(jnp.float32)
                        sides.append(value)
                    reals.append(win_ref[pl.ds(pl.multiple_of(w * BLOCK, BLOCK), BLOCK), :])
                tot_ref[...] = sums
                out_ref[rows, :] += jnp.dot(
                    jnp.concatenate(sides, axis=1),
                    jnp.concatenate(reals, axis=0),
                    preferred_element_type=jnp.float32,
                )
                return carry

            lax.fori_loop(0, (count + 3) // 4, four, 0)
            totals = jnp.sum(tot_ref[...], axis=1, keepdims=True)
            out_ref[rows, :] = totals * sim_ref[rows, :].astype(jnp.float32) - out_ref[rows, :]

    def scaled(e, k, w, rows, valid):
        p = p_ref[e * FAN + k]
        b = jnp.where(valid, b_ref[pl.ds(w, 1), :], 0.0)
        a = a_ref[rows, :]
        return p[:, :LANES] * a * b[:, :LANES], p[:, LANES:] * a * b[:, LANES:]

    def logarithmic(e, k, w, rows, valid):
        t = t_ref[e * FAN + k]
        v = v_ref[pl.ds(w, 1), :] + log_rows
        u = u_ref[rows, :]
        left, right = jnp.exp2(t[:, :LANES] + u + v[:, :LANES]), jnp.exp2(t[:, LANES:] + u + v[:, LANES:])
        return jnp.where(valid, left, 0.0), jnp.where(valid, right, 0.0)

    @pl.when(good)
    def _():
        gather(scaled)

    @pl.when(jnp.logical_not(good))
    def _():
        score_tiles(tab_ref, size_ref, sim_ref, win_ref, n_ref, t_ref, unit)
        gather(logarithmic)


def vmem():
    return pl.BlockSpec(memory_space=pltpu.VMEM)


def smem():
    return pl.BlockSpec(memory_space=pltpu.SMEM)


def shards(sim, real, pair_real, pair_count):
    owners = lax.axis_size("blk")
    features = sim.shape[1]
    local = real.shape[0] // BLOCK
    rows_total = owners * real.shape[0]
    log_rows = math.log2(rows_total)
    unit = LOG2E / EPS / features
    mine = lax.axis_index("blk")
    rep = lax.axis_index("rep")
    fan = pair_real.shape[1]
    group = pair_real // local - mine
    group = jnp.clip(jnp.where(mine % 2 == 0, group + 1, 1 - group), 0, 2)
    table = group * local + pair_real % local
    tiles = 2 * fan
    window = 3 * local
    active = jnp.arange(fan)[None, :] < pair_count[:, None]
    ids = jnp.arange(tiles, dtype=jnp.int32)
    place = jnp.where(active, table // local, 3).reshape(-1)
    rank = jnp.sum((place * tiles + ids)[None, :] < (place * tiles + ids)[:, None], 1)
    order = jnp.sum(jnp.where(rank[:, None] == ids[None, :], ids[:, None], 0), 0)
    bounds = jnp.sum(place[:, None] < jnp.arange(4)[None, :], 0).astype(jnp.int32)
    masks = jnp.where(mine % 2 == 0, jnp.array([0, 1, 3, 2], jnp.int32), jnp.array([0, 3, 1, 2], jnp.int32))
    quarters = rep ^ masks
    sizes = jnp.concatenate([bounds, quarters, pair_count])
    hits = (table[:, :, None] == jnp.arange(window)) & active[:, :, None]
    used = jnp.broadcast_to(jnp.any(hits, (0, 1))[:, None], (window, BLOCK)).astype(jnp.float32)

    own = real
    first = rep_turn(own, (1, 3))
    second = rep_turn(own, (3, 1))
    chip_own = chip_swap(own)
    core_own = core_swap(own)
    first, second, chip_own, core_own, table, order, sizes, used = lax.optimization_barrier(
        (first, second, chip_own, core_own, table, order, sizes, used)
    )
    far = rep_turn(first, (3, 1))
    near = jnp.stack([first, second])
    groups = {
        1: (own, near, far),
        2: (core_own, core_swap(near), core_swap(far)),
        0: (chip_own, chip_swap(near), chip_swap(far)),
    }
    sim_norm = jnp.sum(jnp.square(sim.astype(jnp.float32)), -1) * unit

    stats_shape = jax.ShapeDtypeStruct((window, BLOCK), jnp.float32)
    potentials = (2 * BLOCK, LANES)
    column = jax.ShapeDtypeStruct(potentials, jnp.float32)
    sim_rows = pltpu.with_memory_space_constraint(sim, pltpu.HBM)
    groups[1] = (pltpu.with_memory_space_constraint(own, pltpu.HBM), near, far)
    plans = pltpu.VMEM((tiles, BLOCK, BLOCK), jnp.float32)
    rows_of = pltpu.VMEM((window, BLOCK), jnp.float32)
    sums_of = pltpu.VMEM((window * 8, BLOCK), jnp.float32)
    held_sim = pltpu.VMEM(sim.shape, sim.dtype)
    col = pltpu.VMEM(potentials, jnp.float32)
    held = []
    for group in (1, 2, 0):
        last = group == 0
        found = pl.pallas_call(
            functools.partial(group_kernel, group, log_rows, unit),
            out_shape=[
                plans,
                pltpu.VMEM((window * BLOCK, features), jnp.bfloat16),
                column,
                jax.ShapeDtypeStruct((window * 8, BLOCK), jnp.float32),
                column,
            ]
            + [stats_shape] * last,
            in_specs=[smem()] * 3
            + [pl.BlockSpec(memory_space=pltpu.HBM)]
            + [pl.BlockSpec(memory_space=pltpu.HBM if group == 1 else pl.ANY)]
            + [pl.BlockSpec(memory_space=pl.ANY)] * 2
            + [vmem()] * (last + len(held)),
            out_specs=[vmem()] * (5 + last),
            input_output_aliases={7 + last + i: i for i in range(len(held))},
            scratch_shapes=[col, sums_of, plans, col, rows_of] * last + [held_sim, pltpu.SemaphoreType.DMA((5,))],
            compiler_params=pltpu.CompilerParams(vmem_limit_bytes=(16 if last else 6) * MIB),
            cost_estimate=pl.CostEstimate(flops=10**9, bytes_accessed=8 * MIB, transcendentals=0),
        )(table, order, sizes, sim_rows, *groups[group], *[used] * last, *held)
        held = [pltpu.with_memory_space_constraint(value, pltpu.VMEM) for value in found[:2]] + list(found[2:5])
    plan, window_rows, peaks, norms, _ = held
    stats_out = found[5]

    for sweep in range(ITERS):
        if sweep:
            last = sweep == ITERS - 1
            found = pl.pallas_call(
                functools.partial(sweep_kernel, last, log_rows, unit),
                out_shape=[stats_shape] + [column, jax.ShapeDtypeStruct((2, BLOCK), jnp.float32)] * last,
                in_specs=[smem()] * 2 + [vmem()] * 9 + [pl.BlockSpec(memory_space=pltpu.HBM)],
                out_specs=[vmem()] * (1 + 2 * last),
                scratch_shapes=[col] * (not last)
                + [rows_of, rows_of, col, sums_of, plans, held_sim, pltpu.SemaphoreType.DMA],
                compiler_params=pltpu.CompilerParams(vmem_limit_bytes=14 * MIB),
            )(table, sizes, *around, used, peaks, norms, plan, window_rows, sim_rows)
            stats_out = found[0]
        own_sum = log_add(stats_out[local : 2 * local], core_swap(stats_out[2 * local :]))
        chip = chip_swap(jnp.concatenate([own_sum, stats_out[:local]]))
        own_sum, chip_sum = log_add(own_sum, chip[local:]), log_add(stats_out[:local], chip[:local])
        merged = jnp.concatenate([chip_sum, own_sum, core_swap(own_sum)])
        around = (merged, rep_flip(merged, 1), rep_flip(merged, 3), rep_flip(merged, 2))

    sim_pot, sim_row = found[1:]
    back = EPS / LOG2E
    pull, real_out = pl.pallas_call(
        functools.partial(pull_kernel, log_rows, back, unit),
        out_shape=[
            jax.ShapeDtypeStruct(sim.shape, jnp.float32),
            jax.ShapeDtypeStruct((2 * local, LANES), jnp.float32),
        ],
        in_specs=[smem()] * 2 + [vmem()] * 11,
        out_specs=[vmem()] * 2,
        scratch_shapes=[rows_of, rows_of, col, pltpu.VMEM((BLOCK, LANES), jnp.float32), plans],
        compiler_params=pltpu.CompilerParams(vmem_limit_bytes=16 * MIB),
    )(table, sizes, *around, used, peaks, norms, plan, sim_pot, sim, window_rows)
    sim_out = (sim_row.reshape(-1) + sim_norm) * back
    return (pull, sim_out, real_out.reshape(-1))


def solution(mesh):
    in_specs = (
        P(("blk", "rep"), None),
        P("blk", "rep"),
        P(("blk", "rep"), None),
        P(("blk", "rep")),
    )
    out_specs = (P(("blk", "rep"), None), P(("blk", "rep")), P("blk"))
    return jax.shard_map(shards, mesh=mesh, in_specs=in_specs, out_specs=out_specs, check_vma=False)
```
